256 devices in a mesh: row: 16 (over y_lo, x, core), col: 16 (over y_hi, z).
Axes of the slice: x: 4, y: 4 (y_hi: 2, y_lo: 2; y = y_hi * 2 + y_lo), z: 8, core: 2. Of those that a mesh axis runs over, the one named last changes fastest.
Arguments:
- inputs: bfloat16 [512, 12288], P('col', 'row'), may hold values from -6 to 6
- up_weight: bfloat16 [12288, 24576], P('row', 'col'), may hold values from -0.0546875 to 0.0546875
- down_weight: bfloat16 [24576, 12288], P('col', 'row'), may hold values from -0.078125 to 0.078125
- cotangent: bfloat16 [512, 12288], P('col', 'row'), may hold values from -6 to 6
Outputs:
- outputs: bfloat16 [512, 12288], P('col', 'row')
- input_grad: bfloat16 [512, 12288], P('col', 'row')
- up_grad: bfloat16 [12288, 24576], P('row', 'col')
- down_grad: bfloat16 [24576, 12288], P('col', 'row')
The draws below stay inside these ranges and needn't reach their ends.
All inputs are finite; a program needn't handle non-finite values.
Results may differ from the reference program's by a relative error of at most 0.005.
Values may be sent and summed in bfloat16 or wider, within the bound.
No kernel may reach another device: no remote copies, remote signals or barrier semaphores. Data moves between devices by JAX's collectives and lax.ppermute only.
A program may use at most 64 MiB of HBM per device.

```python
import math
import jax
import jax.numpy as jnp
from jax import lax

D = 12288
FF = 24576
TOKENS = 512


def shard_levels(own_key, shape, split, least, top_value):
    loudness = 1.0
    for position, parts in split:
        draws = jax.random.uniform(jax.random.fold_in(jax.random.fold_in(own_key, 6), position), (parts,), jnp.float32, least / len(split), top_value / len(split))
        loudness = loudness * jnp.repeat(jnp.exp(draws), shape[position] // parts).reshape((-1,) + (1,) * (len(shape) - 1 - position))
    return loudness


def scatter_about(stream_key, extent, spread, most, pieces=(), held_as=jnp.bfloat16):
    values = jax.random.normal(stream_key, extent, jnp.float32) * spread
    if len(pieces) > 0:
        values = shard_levels(stream_key, extent, pieces, -0.22, 0.18) * values
    return jnp.clip(values, min=-most, max=most).astype(held_as)


def setup_inputs(seed: int = 0) -> dict:
    arg_keys = jax.random.split(jax.random.key(seed), 5)
    return {
        "inputs": scatter_about(arg_keys[0], (TOKENS, D), 1.0, 6.0, ((0, 16), (1, 16))),
        "up_weight": scatter_about(arg_keys[1], (D, FF), D ** -0.5, 0.0546875, ((0, 16), (1, 16))),
        "down_weight": scatter_about(arg_keys[2], (FF, D), (FF // 4) ** -0.5, 0.078125, ((0, 16), (1, 16))),
        "cotangent": scatter_about(arg_keys[3], (TOKENS, D), 1.0, 6.0, ((0, 16), (1, 16))),
    }


def gelu_value(v):
    cval = math.sqrt(2.0 / math.pi)
    return 0.5 * v * (1.0 + jnp.tanh(cval * (v + 0.044715 * v * v * v)))

def gelu_slope(v):
    cval = math.sqrt(2.0 / math.pi)
    tval = jnp.tanh(cval * (v + 0.044715 * v * v * v))
    return 0.5 * (1.0 + tval) + 0.5 * v * (1.0 - tval * tval) * cval * (1.0 + 3.0 * 0.044715 * v * v)

def reference(inputs, up_weight, down_weight, cotangent):
    preact = jnp.dot(inputs, up_weight, preferred_element_type=jnp.float32)
    activ = gelu_value(preact).astype(jnp.bfloat16)
    outputs = jnp.dot(activ, down_weight, preferred_element_type=jnp.float32).astype(jnp.bfloat16)
    act_grad = lax.dot_general(cotangent, down_weight, (((1,), (1,)), ((), ())), preferred_element_type=jnp.float32)
    pre_grad = (act_grad * gelu_slope(preact)).astype(jnp.bfloat16)
    down_grad = lax.dot_general(activ, cotangent, (((0,), (0,)), ((), ())), preferred_element_type=jnp.float32).astype(jnp.bfloat16)
    up_grad = lax.dot_general(inputs, pre_grad, (((0,), (0,)), ((), ())), preferred_element_type=jnp.float32).astype(jnp.bfloat16)
    input_grad = lax.dot_general(pre_grad, up_weight, (((1,), (1,)), ((), ())), preferred_element_type=jnp.float32).astype(jnp.bfloat16)
    return (outputs, input_grad, up_grad, down_grad)
```

```python
import math

import jax
import jax.numpy as jnp
from jax import lax
from jax.sharding import PartitionSpec as P

BF16, F32 = jnp.bfloat16, jnp.float32
YL, X, YH, Z = 2, 4, 2, 8


def row_id(yl, x, c):
    return (yl % YL) * 8 + (x % X) * 2 + c % 2


def col_id(yh, z):
    return (yh % YH) * 8 + z % Z


def send_row(value, dyl, dx, dc):
    pairs = [
        (row_id(yl, x, c), row_id(yl + dyl, x + dx, c + dc))
        for yl in range(YL)
        for x in range(X)
        for c in range(2)
    ]
    return lax.ppermute(value, "row", pairs)


def send_col(value, dyh, dz):
    pairs = [
        (col_id(yh, z), col_id(yh + dyh, z + dz)) for yh in range(YH) for z in range(Z)
    ]
    return lax.ppermute(value, "col", pairs)


def send_cross(value):
    pairs = [
        (r * 16 + k, (r ^ 1) * 16 + (k ^ 8)) for r in range(16) for k in range(16)
    ]
    return lax.ppermute(value, ("row", "col"), pairs)


def gelu_value(v):
    cval = math.sqrt(2.0 / math.pi)
    return 0.5 * v * (1.0 + jnp.tanh(cval * (v + 0.044715 * v * v * v)))


def gelu_slope(v):
    cval = math.sqrt(2.0 / math.pi)
    tval = jnp.tanh(cval * (v + 0.044715 * v * v * v))
    return 0.5 * (1.0 + tval) + 0.5 * v * (1.0 - tval * tval) * cval * (
        1.0 + 3.0 * 0.044715 * v * v
    )


def times_transposed(left, right):
    return lax.dot_general(
        left, right, (((1,), (1,)), ((), ())), preferred_element_type=F32
    )


def over_tokens(left, right):
    return lax.dot_general(
        left, right, (((0,), (0,)), ((), ())), preferred_element_type=F32
    )


def rows_at(value, start, count):
    return lax.dynamic_slice_in_dim(value, start, count, axis=0)


def gather_z(own):
    blocks = [None] * Z
    blocks[0] = up = down = own
    for step in range(1, 4):
        up = send_col(up, 0, 1)
        down = send_col(down, 0, -1)
        blocks[Z - step], blocks[step] = up, down
    half = own.shape[0] // 2
    low = send_col(up[:half], 0, 1)
    high = send_col(down[half:], 0, -1)
    blocks[4] = jnp.concatenate([low, high], axis=0)
    return blocks


def scatter_z(part):
    half = part(4).shape[0] // 2
    far = part(4).astype(BF16)
    up = send_col(far[:half], 0, 1)
    down = send_col(far[half:], 0, -1)
    for step in (3, 2, 1):
        goes_up, goes_down = part(step), part(Z - step)
        if step == 3:
            goes_up = jnp.concatenate([goes_up[:half] + up, goes_up[half:]], axis=0)
            goes_down = jnp.concatenate(
                [goes_down[:half], goes_down[half:] + down], axis=0
            )
        else:
            goes_up, goes_down = goes_up + up, goes_down + down
        up = send_col(goes_up.astype(BF16), 0, 1)
        down = send_col(goes_down.astype(BF16), 0, -1)
    return part(0) + up + down


def scatter_x(value, x):
    n = value.shape[0] // X
    total = rows_at(value, x * n, n)
    for d in (1, 2, 3):
        total += send_row(rows_at(value, (x + d) % X * n, n).astype(BF16), 0, d, 0)
    return total


def scatter_y(value, yl):
    n = value.shape[0] // YL
    sent = send_row(rows_at(value, (1 - yl) * n, n).astype(BF16), 1, 0, 0)
    return rows_at(value, yl * n, n) + sent


def gather_x(own):
    return [own] + [send_row(own, 0, -d, 0) for d in (1, 2, 3)]


def per_device(inputs, up_weight, down_weight, cotangent):
    row, col = lax.axis_index("row"), lax.axis_index("col")
    core, x, yl = row % 2, row // 2 % X, row // 8

    both = jnp.stack([inputs, cotangent]).reshape(2, 2, 16, 768)
    mine = lax.dynamic_index_in_dim(both, core, axis=1, keepdims=False)
    other = lax.dynamic_index_in_dim(both, 1 - core, axis=1, keepdims=False)
    got_core = send_row(other, 0, 0, 1)
    got_yh = send_col(mine, 1, 0)
    got_cross = send_cross(other)
    here = jnp.concatenate([mine, got_core], axis=-1)
    there = jnp.concatenate([got_yh, got_cross], axis=-1)
    shard = jnp.concatenate([here, there], axis=1)
    shard, up_own, down_own = lax.optimization_barrier((shard, up_weight, down_weight))

    up_all = jnp.concatenate([up_own, send_row(up_own, 0, 0, 1)], axis=0)
    down_all = jnp.concatenate([down_own, send_row(down_own, 0, 0, 1)], axis=1)

    blocks = gather_z(shard.reshape(64, 1536))
    feats = jnp.concatenate([b[:32] for b in blocks], axis=0)
    cots = jnp.concatenate([b[32:] for b in blocks], axis=0)

    preact_part = jnp.dot(feats, up_all, preferred_element_type=F32)
    act_part = times_transposed(cots, down_all)

    preact = scatter_x(scatter_y(preact_part, yl), x)
    act_half = scatter_x(
        act_part.reshape(YL, X, 32, 1536).swapaxes(0, 1).reshape(256, 1536), x
    )
    act_grad = scatter_y(act_half, yl)

    activ = gelu_value(preact).astype(BF16)
    pre_grad = (act_grad * gelu_slope(preact)).astype(BF16)

    across = jnp.concatenate(gather_x(activ), axis=0)
    activ_all = jnp.concatenate([across, send_row(across, 1, 0, 0)], axis=0)
    pair = jnp.concatenate([pre_grad, send_row(pre_grad, 1, 0, 0)], axis=0)
    pregrad_all = jnp.concatenate(gather_x(pair), axis=0)

    def at_activ(d):
        return ((yl + d // X) % YL * X + (d - x) % X) * 32

    def at_pregrad(d):
        return ((d - x) % X * YL + (yl + d // X) % YL) * 32

    out_part = jnp.dot(activ_all, down_all, preferred_element_type=F32)
    in_part = times_transposed(pregrad_all, up_all)

    def part(d):
        return jnp.concatenate(
            [
                rows_at(out_part, at_activ(d), 32),
                rows_at(in_part, at_pregrad(d), 32),
            ],
            axis=0,
        )

    total = scatter_z(part).reshape(2, 2, 16, 2, 768)
    keep, give = total[:, 0], total[:, 1]
    from_yh = send_col(give[:, :, 0], 1, 0)
    from_core = send_row(keep[:, :, 1], 0, 0, 1)
    from_cross = send_cross(give[:, :, 1])
    mine = keep[:, :, 0] + from_yh
    other = from_core + from_cross
    first = core == 0
    low = jnp.where(first, mine, other)
    high = jnp.where(first, other, mine)
    result = jnp.concatenate([low, high], axis=1).astype(BF16)

    feats_all = jnp.concatenate(
        [feats[:, :768], send_row(feats[:, 768:], 0, 0, 1)], axis=0
    )
    cots_all = jnp.concatenate(
        [cots[:, :768], send_row(cots[:, 768:], 0, 0, 1)], axis=0
    )
    activ_in_order = jnp.concatenate(
        [rows_at(activ_all, at_activ(d), 32) for d in range(Z)], axis=0
    )
    pregrad_in_order = jnp.concatenate(
        [rows_at(pregrad_all, at_pregrad(d), 32) for d in range(Z)], axis=0
    )
    activ_tokens = jnp.concatenate(
        [activ_in_order, send_row(activ_in_order, 0, 0, 1)], axis=0
    )
    pregrad_tokens = jnp.concatenate(
        [pregrad_in_order, send_row(pregrad_in_order, 0, 0, 1)], axis=0
    )
    down_grad = over_tokens(activ_tokens, cots_all).astype(BF16)
    up_grad = over_tokens(feats_all, pregrad_tokens).astype(BF16)
    return (result[0], result[1], up_grad, down_grad)


def solution(mesh):
    placed = (P("col", "row"), P("row", "col"), P("col", "row"), P("col", "row"))
    return jax.shard_map(
        per_device,
        mesh=mesh,
        in_specs=placed,
        out_specs=(P("col", "row"), P("col", "row"), P("row", "col"), P("col", "row")),
        check_vma=False,
    )
```

```python
import math

import jax
import jax.numpy as jnp
from jax import lax
from jax.sharding import PartitionSpec as P

BF16, F32 = jnp.bfloat16, jnp.float32
YL, X, YH, Z = 2, 4, 2, 8


def row_id(yl, x, c):
    return (yl % YL) * 8 + (x % X) * 2 + c % 2


def col_id(yh, z):
    return (yh % YH) * 8 + z % Z


def send_row(value, dyl, dx, dc):
    pairs = [
        (row_id(yl, x, c), row_id(yl + dyl, x + dx, c + dc))
        for yl in range(YL)
        for x in range(X)
        for c in range(2)
    ]
    return lax.ppermute(value, "row", pairs)


def send_col(value, dyh, dz):
    pairs = [
        (col_id(yh, z), col_id(yh + dyh, z + dz)) for yh in range(YH) for z in range(Z)
    ]
    return lax.ppermute(value, "col", pairs)


def gelu_value(v):
    cval = math.sqrt(2.0 / math.pi)
    return 0.5 * v * (1.0 + jnp.tanh(cval * (v + 0.044715 * v * v * v)))


def gelu_slope(v):
    cval = math.sqrt(2.0 / math.pi)
    tval = jnp.tanh(cval * (v + 0.044715 * v * v * v))
    return 0.5 * (1.0 + tval) + 0.5 * v * (1.0 - tval * tval) * cval * (
        1.0 + 3.0 * 0.044715 * v * v
    )


def times_transposed(left, right):
    return lax.dot_general(
        left, right, (((1,), (1,)), ((), ())), preferred_element_type=F32
    )


def over_tokens(left, right):
    return lax.dot_general(
        left, right, (((0,), (0,)), ((), ())), preferred_element_type=F32
    )


def rows_at(value, start, count):
    return lax.dynamic_slice_in_dim(value, start, count, axis=0)


def gather_z(own):
    blocks = [None] * Z
    blocks[0] = up = down = own
    half = own.shape[0] // 2
    for step in (1, 2, 3, 4):
        if step == 4:
            up, down = up[:half], down[half:]
        up, down = lax.optimization_barrier((up, down))
        up, down = send_col(up, 0, 1), send_col(down, 0, -1)
        up, down = lax.optimization_barrier((up, down))
        blocks[Z - step], blocks[step] = up, down
    blocks[4] = jnp.concatenate([up, down], axis=0)
    return blocks


def scatter_z(part, beside):
    n = part(4).shape[0]
    half = n // 2
    far = part(4).astype(BF16)
    up, down, done = far[:half], far[half:], []
    for step in (4, 3, 2, 1):
        if step == 3:
            nothing = jnp.zeros((n - half, up.shape[1]), F32)
            up = jnp.concatenate([up.astype(F32), nothing], axis=0)
            down = jnp.concatenate([nothing, down.astype(F32)], axis=0)
        if step < 4:
            up = (part(step) + up).astype(BF16)
            down = (part(Z - step) + down).astype(BF16)
        up, down = lax.optimization_barrier((up, down))
        up, down = send_col(up, 0, 1), send_col(down, 0, -1)
        if beside:
            done.append(beside.pop(0)(*done))
        up, down, done = lax.optimization_barrier((up, down, done))
    return part(0) + up + down, done


def x_terms(value, x):
    n = value.shape[0] // X
    return [rows_at(value, (x + d) % X * n, n).astype(BF16) for d in (1, 2, 3)]


def scatter_x(value, x, terms):
    n = value.shape[0] // X
    total = rows_at(value, x * n, n)
    for d in (2, 1, 3):
        total += send_row(terms[d - 1], 0, d, 0)
    return total


def y_term(value, yl):
    n = value.shape[0] // YL
    return rows_at(value, (1 - yl) * n, n)


def scatter_y(value, yl, term):
    n = value.shape[0] // YL
    return rows_at(value, yl * n, n) + send_row(term, 1, 0, 0)


def gather_x(own):
    far = send_row(own, 0, -2, 0)
    return [own, send_row(own, 0, -1, 0), far, send_row(own, 0, -3, 0)]


def per_device(inputs, up_weight, down_weight, cotangent):
    row, col = lax.axis_index("row"), lax.axis_index("col")
    core, x, yl = row % 2, row // 2 % X, row // 8

    both = jnp.stack([inputs, cotangent]).reshape(2, 2, 16, 768)
    mine = lax.dynamic_index_in_dim(both, core, axis=1, keepdims=False)
    other = lax.dynamic_index_in_dim(both, 1 - core, axis=1, keepdims=False)
    here = jnp.concatenate([mine, send_row(other, 0, 0, 1)], axis=-1)
    there = send_col(here, 1, 0)
    shard = jnp.concatenate([here, there], axis=1)
    shard, up_own, down_own = lax.optimization_barrier((shard, up_weight, down_weight))

    up_all = jnp.concatenate([up_own, send_row(up_own, 0, 0, 1)], axis=0)
    down_all = jnp.concatenate([down_own, send_row(down_own, 0, 0, 1)], axis=1)

    blocks = gather_z(shard.reshape(64, 1536))
    feats = jnp.concatenate([b[:32] for b in blocks], axis=0)
    cots = jnp.concatenate([b[32:] for b in blocks], axis=0)

    preact_part = jnp.dot(feats, up_all, preferred_element_type=F32)
    to_y = y_term(preact_part, yl).astype(BF16)
    act_part = times_transposed(cots, down_all)
    act_part = act_part.reshape(YL, X, 32, 1536).swapaxes(0, 1).reshape(256, 1536)
    to_x = x_terms(act_part, x)
    pre_half = scatter_y(preact_part, yl, to_y)
    act_half = scatter_x(act_part, x, to_x)
    preact = scatter_x(pre_half, x, x_terms(pre_half, x))
    act_grad = scatter_y(act_half, yl, y_term(act_half, yl))

    activ = gelu_value(preact).astype(BF16)
    pre_grad = (act_grad * gelu_slope(preact)).astype(BF16)

    across = jnp.concatenate(gather_x(activ), axis=0)
    pair = jnp.concatenate([pre_grad, send_row(pre_grad, 1, 0, 0)], axis=0)
    across, pair = lax.optimization_barrier((across, pair))
    activ_all = jnp.concatenate([across, send_row(across, 1, 0, 0)], axis=0)
    pregrad_all = jnp.concatenate(gather_x(pair), axis=0)

    def at_activ(d):
        return ((yl + d // X) % YL * X + (d - x) % X) * 32

    def at_pregrad(d):
        return ((d - x) % X * YL + (yl + d // X) % YL) * 32

    out_part = jnp.dot(activ_all, down_all, preferred_element_type=F32)
    in_part = times_transposed(pregrad_all, up_all)

    def part(d):
        return jnp.concatenate(
            [
                rows_at(out_part, at_activ(d), 32),
                rows_at(in_part, at_pregrad(d), 32),
            ],
            axis=0,
        )

    feats_other, cots_other, activ_late, pregrad_late = lax.optimization_barrier(
        (feats[:, 768:], cots[:, 768:], activ_all, pregrad_all)
    )

    def exchange():
        activ_in_order = jnp.concatenate(
            [rows_at(activ_late, at_activ(d), 32) for d in range(Z)], axis=0
        )
        pregrad_in_order = jnp.concatenate(
            [rows_at(pregrad_late, at_pregrad(d), 32) for d in range(Z)], axis=0
        )
        own = (feats[:, :768], cots[:, :768], activ_in_order, pregrad_in_order)
        give = (feats_other, cots_other, activ_in_order, pregrad_in_order)
        return [
            jnp.concatenate([a, send_row(b, 0, 0, 1)], axis=0)
            for a, b in zip(own, give)
        ]

    def down_gradient(tokens):
        return over_tokens(tokens[2], tokens[1]).astype(BF16)

    def up_gradient(tokens, down_grad):
        return over_tokens(tokens[0], tokens[3]).astype(BF16)

    total, (_, down_grad, up_grad) = scatter_z(
        part, [exchange, down_gradient, up_gradient]
    )
    total = total.reshape(2, 2, 16, 1536)
    total = total[:, 0] + send_col(total[:, 1], 1, 0)
    mine = total[:, :, :768]
    other = send_row(total[:, :, 768:], 0, 0, 1)
    first = core == 0
    low = jnp.where(first, mine, other)
    high = jnp.where(first, other, mine)
    result = jnp.concatenate([low, high], axis=1).astype(BF16)
    return (result[0], result[1], up_grad, down_grad)


def solution(mesh):
    placed = (P("col", "row"), P("row", "col"), P("col", "row"), P("col", "row"))
    return jax.shard_map(
        per_device,
        mesh=mesh,
        in_specs=placed,
        out_specs=(P("col", "row"), P("col", "row"), P("row", "col"), P("col", "row")),
        check_vma=False,
    )
```

```python
import math

import jax
import jax.numpy as jnp
from jax import lax
from jax.sharding import PartitionSpec as P

BF16, F32 = jnp.bfloat16, jnp.float32
YL, X, YH, Z = 2, 4, 2, 8


def row_id(yl, x, c):
    return (yl % YL) * 8 + (x % X) * 2 + c % 2


def col_id(yh, z):
    return (yh % YH) * 8 + z % Z


def send_row(value, dyl, dx, dc):
    pairs = [
        (row_id(yl, x, c), row_id(yl + dyl, x + dx, c + dc))
        for yl in range(YL)
        for x in range(X)
        for c in range(2)
    ]
    return lax.ppermute(value, "row", pairs)


def send_col(value, dyh, dz):
    pairs = [
        (col_id(yh, z), col_id(yh + dyh, z + dz)) for yh in range(YH) for z in range(Z)
    ]
    return lax.ppermute(value, "col", pairs)


def gelu_value(v):
    cval = math.sqrt(2.0 / math.pi)
    return 0.5 * v * (1.0 + jnp.tanh(cval * (v + 0.044715 * v * v * v)))


def gelu_slope(v):
    cval = math.sqrt(2.0 / math.pi)
    tval = jnp.tanh(cval * (v + 0.044715 * v * v * v))
    return 0.5 * (1.0 + tval) + 0.5 * v * (1.0 - tval * tval) * cval * (
        1.0 + 3.0 * 0.044715 * v * v
    )


def times_transposed(left, right):
    return lax.dot_general(
        left, right, (((1,), (1,)), ((), ())), preferred_element_type=F32
    )


def over_tokens(left, right):
    return lax.dot_general(
        left, right, (((0,), (0,)), ((), ())), preferred_element_type=F32
    )


def rows_at(value, start, count):
    return lax.dynamic_slice_in_dim(value, start, count, axis=0)


def gather_z(own):
    blocks = [None] * Z
    blocks[0] = up = down = own
    half = own.shape[0] // 2
    for step in (1, 2, 3, 4):
        if step == 4:
            up, down = up[:half], down[half:]
        up, down = lax.optimization_barrier((up, down))
        up, down = send_col(up, 0, 1), send_col(down, 0, -1)
        up, down = lax.optimization_barrier((up, down))
        blocks[Z - step], blocks[step] = up, down
    blocks[4] = jnp.concatenate([up, down], axis=0)
    return blocks


def scatter_z(part, beside):
    n = part(4).shape[0]
    half = n // 2
    far = part(4).astype(BF16)
    up, down, done = far[:half], far[half:], []
    for step in (4, 3, 2, 1):
        if step == 3:
            nothing = jnp.zeros((n - half, up.shape[1]), F32)
            up = jnp.concatenate([up.astype(F32), nothing], axis=0)
            down = jnp.concatenate([nothing, down.astype(F32)], axis=0)
        if step < 4:
            up = (part(step) + up).astype(BF16)
            down = (part(Z - step) + down).astype(BF16)
        up, down = lax.optimization_barrier((up, down))
        up, down = send_col(up, 0, 1), send_col(down, 0, -1)
        if beside:
            done.append(beside.pop(0)(*done))
        up, down, done = lax.optimization_barrier((up, down, done))
    return part(0) + up + down, done


def x_terms(value, x):
    n = value.shape[0] // X
    return [rows_at(value, (x + d) % X * n, n).astype(BF16) for d in (1, 2, 3)]


def scatter_x(value, x, terms):
    n = value.shape[0] // X
    total = rows_at(value, x * n, n)
    for d in (2, 1, 3):
        total += send_row(terms[d - 1], 0, d, 0)
    return total


def y_term(value, yl):
    n = value.shape[0] // YL
    return rows_at(value, (1 - yl) * n, n)


def scatter_y(value, yl, term):
    n = value.shape[0] // YL
    return rows_at(value, yl * n, n) + send_row(term, 1, 0, 0)


def gather_x(own):
    far = send_row(own, 0, -2, 0)
    return [own, send_row(own, 0, -1, 0), far, send_row(own, 0, -3, 0)]


def per_device(inputs, up_weight, down_weight, cotangent):
    row, col = lax.axis_index("row"), lax.axis_index("col")
    core, x, yl = row % 2, row // 2 % X, row // 8

    both = jnp.stack([inputs, cotangent]).reshape(2, 2, 16, 768)
    mine = lax.dynamic_index_in_dim(both, core, axis=1, keepdims=False)
    other = lax.dynamic_index_in_dim(both, 1 - core, axis=1, keepdims=False)
    here = jnp.concatenate([mine, send_row(other, 0, 0, 1)], axis=-1)
    there = send_col(here, 1, 0)
    shard = jnp.concatenate([here, there], axis=1)
    shard, up_own, down_own = lax.optimization_barrier((shard, up_weight, down_weight))

    up_all = jnp.concatenate([up_own, send_row(up_own, 0, 0, 1)], axis=0)
    down_all = jnp.concatenate([down_own, send_row(down_own, 0, 0, 1)], axis=1)

    blocks = gather_z(shard.reshape(64, 1536))
    feats = jnp.concatenate([b[:32] for b in blocks], axis=0)
    cots = jnp.concatenate([b[32:] for b in blocks], axis=0)

    preact_part = jnp.dot(feats, up_all, preferred_element_type=F32)
    to_y = y_term(preact_part, yl).astype(BF16)
    act_part = times_transposed(cots, down_all)
    act_part = act_part.reshape(YL, X, 32, 1536).swapaxes(0, 1).reshape(256, 1536)
    to_x = x_terms(act_part, x)
    pre_half = scatter_y(preact_part, yl, to_y)
    act_half = scatter_x(act_part, x, to_x)
    preact = scatter_x(pre_half, x, x_terms(pre_half, x))
    act_grad = scatter_y(act_half, yl, y_term(act_half, yl))

    activ = gelu_value(preact).astype(BF16)
    pre_grad = (act_grad * gelu_slope(preact)).astype(BF16)

    across = jnp.concatenate(gather_x(activ), axis=0)
    pair = jnp.concatenate([pre_grad, send_row(pre_grad, 1, 0, 0)], axis=0)
    across, pair = lax.optimization_barrier((across, pair))
    activ_all = jnp.concatenate([across, send_row(across, 1, 0, 0)], axis=0)
    pairs = gather_x(pair)
    pregrad_all = jnp.concatenate(pairs, axis=0)

    def at_activ(d):
        return ((yl + d // X) % YL * X + (d - x) % X) * 32

    def at_pregrad(d):
        return ((d - x) % X * YL + (yl + d // X) % YL) * 32

    def out_rows(rows):
        return jnp.dot(rows, down_all, preferred_element_type=F32)

    def in_rows(rows):
        return times_transposed(rows, up_all)

    first_block = jnp.concatenate(
        [
            out_rows(rows_at(activ_all, at_activ(4), 32)),
            in_rows(rows_at(pregrad_all, at_pregrad(4), 32)),
        ],
        axis=0,
    )
    out_part = out_rows(activ_all)
    first_block, pair_rows = lax.optimization_barrier((first_block, pairs[0]))
    in_part = in_rows(jnp.concatenate([pair_rows] + pairs[1:], axis=0))

    def part(d):
        if d == 4:
            return first_block
        return jnp.concatenate(
            [
                rows_at(out_part, at_activ(d), 32),
                rows_at(in_part, at_pregrad(d), 32),
            ],
            axis=0,
        )

    def exchange():
        activ_in_order = [rows_at(activ_all, at_activ(d), 32) for d in range(Z)]
        pregrad_in_order = [rows_at(pregrad_all, at_pregrad(d), 32) for d in range(Z)]
        given = jnp.concatenate([feats[:, 768:], cots[:, 768:]], axis=1)
        given = jnp.concatenate([given] + activ_in_order + pregrad_in_order, axis=0)
        got = send_row(given, 0, 0, 1)
        return [
            jnp.concatenate([feats[:, :768], got[:256, :768]], axis=0),
            jnp.concatenate([cots[:, :768], got[:256, 768:]], axis=0),
            jnp.concatenate([given[256:512], got[256:512]], axis=0),
            jnp.concatenate([given[512:], got[512:]], axis=0),
        ]

    def down_gradient(tokens):
        return over_tokens(tokens[2], tokens[1]).astype(BF16)

    def up_gradient(tokens, down_grad):
        return over_tokens(tokens[0], tokens[3]).astype(BF16)

    total, (_, down_grad, up_grad) = scatter_z(
        part, [exchange, down_gradient, up_gradient]
    )
    total = total.reshape(2, 2, 16, 1536)
    total = total[:, 0] + send_col(total[:, 1].astype(BF16), 1, 0)
    mine = total[:, :, :768]
    other = send_row(total[:, :, 768:], 0, 0, 1)
    first = core == 0
    low = jnp.where(first, mine, other)
    high = jnp.where(first, other, mine)
    result = jnp.concatenate([low, high], axis=1).astype(BF16)
    return (result[0], result[1], up_grad, down_grad)


def solution(mesh):
    placed = (P("col", "row"), P("row", "col"), P("col", "row"), P("col", "row"))
    return jax.shard_map(
        per_device,
        mesh=mesh,
        in_specs=placed,
        out_specs=(P("col", "row"), P("col", "row"), P("row", "col"), P("col", "row")),
        check_vma=False,
    )
```

```python
import math

import jax
import jax.numpy as jnp
from jax import lax
from jax.sharding import PartitionSpec as P

BF16, F32 = jnp.bfloat16, jnp.float32
YL, X, YH, Z = 2, 4, 2, 8


def row_id(yl, x, c):
    return (yl % YL) * 8 + (x % X) * 2 + c % 2


def col_id(yh, z):
    return (yh % YH) * 8 + z % Z


def send_row(value, dyl, dx, dc):
    pairs = [
        (row_id(yl, x, c), row_id(yl + dyl, x + dx, c + dc))
        for yl in range(YL)
        for x in range(X)
        for c in range(2)
    ]
    return lax.ppermute(value, "row", pairs)


def send_col(value, dyh, dz):
    pairs = [
        (col_id(yh, z), col_id(yh + dyh, z + dz)) for yh in range(YH) for z in range(Z)
    ]
    return lax.ppermute(value, "col", pairs)


def gelu_value(v):
    cval = math.sqrt(2.0 / math.pi)
    return 0.5 * v * (1.0 + jnp.tanh(cval * (v + 0.044715 * v * v * v)))


def gelu_slope(v):
    cval = math.sqrt(2.0 / math.pi)
    tval = jnp.tanh(cval * (v + 0.044715 * v * v * v))
    return 0.5 * (1.0 + tval) + 0.5 * v * (1.0 - tval * tval) * cval * (
        1.0 + 3.0 * 0.044715 * v * v
    )


def times_transposed(left, right):
    return lax.dot_general(
        left, right, (((1,), (1,)), ((), ())), preferred_element_type=F32
    )


def over_tokens(left, right):
    return lax.dot_general(
        left, right, (((0,), (0,)), ((), ())), preferred_element_type=F32
    )


def rows_at(value, start, count):
    return lax.dynamic_slice_in_dim(value, start, count, axis=0)


def gather_z(own):
    blocks = [None] * Z
    blocks[0] = up = down = own
    half = own.shape[0] // 2
    for step in (1, 2, 3, 4):
        if step == 4:
            up, down = up[:half], down[half:]
        up, down = lax.optimization_barrier((up, down))
        up, down = send_col(up, 0, 1), send_col(down, 0, -1)
        up, down = lax.optimization_barrier((up, down))
        blocks[Z - step], blocks[step] = up, down
    blocks[4] = jnp.concatenate([up, down], axis=0)
    return blocks


def scatter_z(part, piece, exchange, gradient):
    n = part(4).shape[0]
    half = n // 2
    far = part(4).astype(BF16)
    up, down, given, done = far[:half], far[half:], None, None
    for step in (4, 3, 2, 1):
        if step == 3:
            nothing = jnp.zeros((n - half, up.shape[1]), F32)
            up = jnp.concatenate([up.astype(F32), nothing], axis=0)
            down = jnp.concatenate([nothing, down.astype(F32)], axis=0)
        if step < 4:
            up = (part(step) + up).astype(BF16)
            down = (part(Z - step) + down).astype(BF16)
        up, down = lax.optimization_barrier((up, down))
        up, down = send_col(up, 0, 1), send_col(down, 0, -1)
        if step == 3:
            up, down, piece = lax.optimization_barrier((up, down, piece))
        elif step == 2:
            given = exchange(piece)
            up, down, given = lax.optimization_barrier((up, down, given))
        elif step == 1:
            done = gradient(given)
            up, down, done = lax.optimization_barrier((up, down, done))
        else:
            up, down = lax.optimization_barrier((up, down))
    return part(0) + up + down, given, done


def x_terms(value, x):
    n = value.shape[0] // X
    return [rows_at(value, (x + d) % X * n, n).astype(BF16) for d in (1, 2, 3)]


def scatter_x(value, x, terms):
    n = value.shape[0] // X
    total = rows_at(value, x * n, n)
    for d in (2, 1, 3):
        total += send_row(terms[d - 1], 0, d, 0)
    return total


def y_term(value, yl):
    n = value.shape[0] // YL
    return rows_at(value, (1 - yl) * n, n)


def scatter_y(value, yl, term):
    n = value.shape[0] // YL
    return rows_at(value, yl * n, n) + send_row(term, 1, 0, 0)


def gather_x(own):
    far = send_row(own, 0, -2, 0)
    return [own, send_row(own, 0, -1, 0), far, send_row(own, 0, -3, 0)]


def per_device(inputs, up_weight, down_weight, cotangent):
    row, col = lax.axis_index("row"), lax.axis_index("col")
    core, x, yl = row % 2, row // 2 % X, row // 8

    both = jnp.stack([inputs, cotangent]).reshape(2, 2, 16, 768)
    mine = lax.dynamic_index_in_dim(both, core, axis=1, keepdims=False)
    other = lax.dynamic_index_in_dim(both, 1 - core, axis=1, keepdims=False)
    here = jnp.concatenate([mine, send_row(other, 0, 0, 1)], axis=-1)
    there = send_col(here, 1, 0)
    shard = jnp.concatenate([here, there], axis=1)
    shard, up_own, down_own = lax.optimization_barrier((shard, up_weight, down_weight))

    up_all = jnp.concatenate([up_own, send_row(up_own, 0, 0, 1)], axis=0)
    down_all = jnp.concatenate([down_own, send_row(down_own, 0, 0, 1)], axis=1)

    blocks = gather_z(shard.reshape(64, 1536))
    feats = jnp.concatenate([b[:32] for b in blocks], axis=0)
    cots = jnp.concatenate([b[32:] for b in blocks], axis=0)

    preact_part = jnp.dot(feats, up_all, preferred_element_type=F32)
    to_y = y_term(preact_part, yl).astype(BF16)
    act_part = times_transposed(cots, down_all)
    act_part = act_part.reshape(YL, X, 32, 1536).swapaxes(0, 1).reshape(256, 1536)
    to_x = x_terms(act_part, x)
    pre_half = scatter_y(preact_part, yl, to_y)
    act_half = scatter_x(act_part, x, to_x)
    preact = scatter_x(pre_half, x, x_terms(pre_half, x))
    act_grad = scatter_y(act_half, yl, y_term(act_half, yl))

    activ = gelu_value(preact).astype(BF16)
    pre_grad = (act_grad * gelu_slope(preact)).astype(BF16)

    across = jnp.concatenate(gather_x(activ), axis=0)
    pair = jnp.concatenate([pre_grad, send_row(pre_grad, 1, 0, 0)], axis=0)
    across, pair = lax.optimization_barrier((across, pair))
    activ_all = jnp.concatenate([across, send_row(across, 1, 0, 0)], axis=0)
    pairs = gather_x(pair)
    pregrad_all = jnp.concatenate(pairs, axis=0)

    def at_activ(d):
        return ((yl + d // X) % YL * X + (d - x) % X) * 32

    def at_pregrad(d):
        return ((d - x) % X * YL + (yl + d // X) % YL) * 32

    def out_rows(rows):
        return jnp.dot(rows, down_all, preferred_element_type=F32)

    def in_rows(rows):
        return times_transposed(rows, up_all)

    first_block = jnp.concatenate(
        [
            out_rows(rows_at(activ_all, at_activ(4), 32)),
            in_rows(rows_at(pregrad_all, at_pregrad(4), 32)),
        ],
        axis=0,
    )
    out_part = out_rows(activ_all)
    first_block, pair_rows = lax.optimization_barrier((first_block, pairs[0]))
    in_part = in_rows(jnp.concatenate([pair_rows] + pairs[1:], axis=0))

    def part(d):
        if d == 4:
            return first_block
        return jnp.concatenate(
            [
                rows_at(out_part, at_activ(d), 32),
                rows_at(in_part, at_pregrad(d), 32),
            ],
            axis=0,
        )

    def exchange(piece):
        activ_in_order = [piece]
        activ_in_order += [rows_at(activ_all, at_activ(d), 32) for d in range(1, Z)]
        pregrad_in_order = [rows_at(pregrad_all, at_pregrad(d), 32) for d in range(Z)]
        given = jnp.concatenate([feats[:, 768:], cots[:, 768:]], axis=1)
        given = jnp.concatenate([given] + activ_in_order + pregrad_in_order, axis=0)
        got = send_row(given, 0, 0, 1)
        return [
            jnp.concatenate([feats[:, :768], got[:256, :768]], axis=0),
            jnp.concatenate([cots[:, :768], got[:256, 768:]], axis=0),
            jnp.concatenate([given[256:512], got[256:512]], axis=0),
            jnp.concatenate([given[512:], got[512:]], axis=0),
        ]

    def down_gradient(tokens):
        return over_tokens(tokens[2], tokens[1]).astype(BF16)

    total, tokens, down_grad = scatter_z(
        part, rows_at(activ_all, at_activ(0), 32), exchange, down_gradient
    )
    total = total.reshape(2, 2, 16, 1536)
    other = send_col(total[:, 1].astype(BF16), 1, 0)
    up_grad = over_tokens(tokens[0], tokens[3]).astype(BF16)
    other, up_grad = lax.optimization_barrier((other, up_grad))
    total = total[:, 0] + other
    mine = total[:, :, :768]
    other = send_row(total[:, :, 768:], 0, 0, 1)
    first = core == 0
    low = jnp.where(first, mine, other)
    high = jnp.where(first, other, mine)
    result = jnp.concatenate([low, high], axis=1).astype(BF16)
    return (result[0], result[1], up_grad, down_grad)


def solution(mesh):
    placed = (P("col", "row"), P("row", "col"), P("col", "row"), P("col", "row"))
    return jax.shard_map(
        per_device,
        mesh=mesh,
        in_specs=placed,
        out_specs=(P("col", "row"), P("col", "row"), P("row", "col"), P("col", "row")),
        check_vma=False,
    )
```

```python
import math

import jax
import jax.numpy as jnp
from jax import lax
from jax.sharding import PartitionSpec as P

BF16, F32 = jnp.bfloat16, jnp.float32
YL, X, YH, Z = 2, 4, 2, 8


def row_id(yl, x, c):
    return (yl % YL) * 8 + (x % X) * 2 + c % 2


def col_id(yh, z):
    return (yh % YH) * 8 + z % Z


def send_row(value, dyl, dx, dc):
    pairs = [
        (row_id(yl, x, c), row_id(yl + dyl, x + dx, c + dc))
        for yl in range(YL)
        for x in range(X)
        for c in range(2)
    ]
    return lax.ppermute(value, "row", pairs)


def send_col(value, dyh, dz):
    pairs = [
        (col_id(yh, z), col_id(yh + dyh, z + dz)) for yh in range(YH) for z in range(Z)
    ]
    return lax.ppermute(value, "col", pairs)


def gelu_value(v):
    cval = math.sqrt(2.0 / math.pi)
    return 0.5 * v * (1.0 + jnp.tanh(cval * (v + 0.044715 * v * v * v)))


def gelu_slope(v):
    cval = math.sqrt(2.0 / math.pi)
    tval = jnp.tanh(cval * (v + 0.044715 * v * v * v))
    return 0.5 * (1.0 + tval) + 0.5 * v * (1.0 - tval * tval) * cval * (
        1.0 + 3.0 * 0.044715 * v * v
    )


def times_transposed(left, right):
    return lax.dot_general(
        left, right, (((1,), (1,)), ((), ())), preferred_element_type=F32
    )


def over_tokens(left, right):
    return lax.dot_general(
        left, right, (((0,), (0,)), ((), ())), preferred_element_type=F32
    )


def rows_at(value, start, count):
    return lax.dynamic_slice_in_dim(value, start, count, axis=0)


def gather_z(own):
    blocks = [None] * Z
    blocks[0] = up = down = own
    half = own.shape[0] // 2
    for step in (1, 2, 3, 4):
        if step == 4:
            up, down = up[:half], down[half:]
        up, down = lax.optimization_barrier((up, down))
        up, down = send_col(up, 0, 1), send_col(down, 0, -1)
        up, down = lax.optimization_barrier((up, down))
        blocks[Z - step], blocks[step] = up, down
    blocks[4] = jnp.concatenate([up, down], axis=0)
    return blocks


def scatter_z(part, beside):
    n = part(4).shape[0]
    half = n // 2
    far = part(4).astype(BF16)
    up, down, done = far[:half], far[half:], []
    for step in (4, 3, 2, 1):
        if step == 3:
            nothing = jnp.zeros((n - half, up.shape[1]), F32)
            up = jnp.concatenate([up.astype(F32), nothing], axis=0)
            down = jnp.concatenate([nothing, down.astype(F32)], axis=0)
        if step < 4:
            up = (part(step) + up).astype(BF16)
            down = (part(Z - step) + down).astype(BF16)
        up, down = lax.optimization_barrier((up, down))
        up, down = send_col(up, 0, 1), send_col(down, 0, -1)
        if beside:
            done.append(beside.pop(0)(*done))
        up, down, done = lax.optimization_barrier((up, down, done))
    return part(0) + up + down, done


def x_terms(value, x):
    n = value.shape[0] // X
    return [rows_at(value, (x + d) % X * n, n).astype(BF16) for d in (1, 2, 3)]


def scatter_x(value, x, terms):
    n = value.shape[0] // X
    total = rows_at(value, x * n, n)
    for d in (1, 3, 2):
        total += send_row(terms[d - 1], 0, d, 0)
    return total


def y_term(value, yl):
    n = value.shape[0] // YL
    return rows_at(value, (1 - yl) * n, n)


def scatter_y(value, yl, term):
    n = value.shape[0] // YL
    return rows_at(value, yl * n, n) + send_row(term, 1, 0, 0)


def gather_x(own):
    return [own] + [send_row(own, 0, -d, 0) for d in (1, 3, 2)]


def x_place(d):
    return d ^ (d >> 1)


def per_device(inputs, up_weight, down_weight, cotangent):
    row, col = lax.axis_index("row"), lax.axis_index("col")
    core, x, yl = row % 2, row // 2 % X, row // 8

    both = jnp.stack([inputs, cotangent]).reshape(2, 2, 16, 768)
    mine = lax.dynamic_index_in_dim(both, core, axis=1, keepdims=False)
    other = lax.dynamic_index_in_dim(both, 1 - core, axis=1, keepdims=False)
    here = jnp.concatenate([mine, send_row(other, 0, 0, 1)], axis=-1)
    there = send_col(here, 1, 0)
    shard = jnp.concatenate([here, there], axis=1)
    shard, up_own, down_own = lax.optimization_barrier((shard, up_weight, down_weight))

    up_all = jnp.concatenate([up_own, send_row(up_own, 0, 0, 1)], axis=0)
    down_all = jnp.concatenate([down_own, send_row(down_own, 0, 0, 1)], axis=1)

    blocks = gather_z(shard.reshape(64, 1536))
    feats = jnp.concatenate([b[:32] for b in blocks], axis=0)
    cots = jnp.concatenate([b[32:] for b in blocks], axis=0)

    preact_part = jnp.dot(feats, up_all, preferred_element_type=F32)
    to_y = y_term(preact_part, yl).astype(BF16)
    act_part = times_transposed(cots, down_all)
    act_part = act_part.reshape(YL, X, 32, 1536).swapaxes(0, 1).reshape(256, 1536)
    to_x = x_terms(act_part, x)
    pre_half = scatter_y(preact_part, yl, to_y)
    act_half = scatter_x(act_part, x, to_x)
    preact = scatter_x(pre_half, x, x_terms(pre_half, x))
    act_grad = scatter_y(act_half, yl, y_term(act_half, yl))

    activ = gelu_value(preact).astype(BF16)
    pre_grad = (act_grad * gelu_slope(preact)).astype(BF16)

    across = jnp.concatenate(gather_x(activ), axis=0)
    pair = jnp.concatenate([pre_grad, send_row(pre_grad, 1, 0, 0)], axis=0)
    across, pair = lax.optimization_barrier((across, pair))
    pairs = gather_x(pair)
    pregrad_all = jnp.concatenate(pairs, axis=0)
    activ_all = jnp.concatenate([across, send_row(across, 1, 0, 0)], axis=0)

    def at_activ(d):
        return ((yl + d // X) % YL * X + x_place((d - x) % X)) * 32

    def at_pregrad(d):
        return (x_place((d - x) % X) * YL + (yl + d // X) % YL) * 32

    def out_rows(rows):
        return jnp.dot(rows, down_all, preferred_element_type=F32)

    def in_rows(rows):
        return times_transposed(rows, up_all)

    first_block = jnp.concatenate(
        [
            in_rows(rows_at(pregrad_all, at_pregrad(4), 32)),
            out_rows(rows_at(activ_all, at_activ(4), 32)),
        ],
        axis=0,
    )
    out_part = out_rows(activ_all)
    first_block, pair_rows = lax.optimization_barrier((first_block, pairs[0]))
    in_part = in_rows(jnp.concatenate([pair_rows] + pairs[1:], axis=0))

    def part(d):
        if d == 4:
            return first_block
        return jnp.concatenate(
            [
                rows_at(in_part, at_pregrad(d), 32),
                rows_at(out_part, at_activ(d), 32),
            ],
            axis=0,
        )

    def exchange():
        activ_in_order = [rows_at(activ_all, at_activ(d), 32) for d in range(Z)]
        pregrad_in_order = [rows_at(pregrad_all, at_pregrad(d), 32) for d in range(Z)]
        given = jnp.concatenate([feats[:, 768:], cots[:, 768:]], axis=1)
        given = jnp.concatenate([given] + activ_in_order + pregrad_in_order, axis=0)
        got = send_row(given, 0, 0, 1)
        return [
            jnp.concatenate([feats[:, :768], got[:256, :768]], axis=0),
            jnp.concatenate([cots[:, :768], got[:256, 768:]], axis=0),
            jnp.concatenate([given[256:512], got[256:512]], axis=0),
            jnp.concatenate([given[512:], got[512:]], axis=0),
        ]

    def down_gradient(tokens):
        return over_tokens(tokens[2], tokens[1]).astype(BF16)

    def up_gradient(tokens, down_grad):
        return over_tokens(tokens[0], tokens[3]).astype(BF16)

    total, (_, down_grad, up_grad) = scatter_z(
        part, [exchange, down_gradient, up_gradient]
    )
    total = total.reshape(2, 2, 16, 1536)
    total = total[:, 0] + send_col(total[:, 1].astype(BF16), 1, 0)
    mine = total[:, :, :768]
    other = send_row(total[:, :, 768:], 0, 0, 1)
    first = core == 0
    low = jnp.where(first, mine, other)
    high = jnp.where(first, other, mine)
    result = jnp.concatenate([low, high], axis=1).astype(BF16)
    return (result[1], result[0], up_grad, down_grad)


def solution(mesh):
    placed = (P("col", "row"), P("row", "col"), P("col", "row"), P("col", "row"))
    return jax.shard_map(
        per_device,
        mesh=mesh,
        in_specs=placed,
        out_specs=(P("col", "row"), P("col", "row"), P("row", "col"), P("col", "row")),
        check_vma=False,
    )
```

```python
import math

import jax
import jax.numpy as jnp
from jax import lax
from jax.sharding import PartitionSpec as P

BF16, F32 = jnp.bfloat16, jnp.float32
YL, X, YH, Z = 2, 4, 2, 8


def row_id(yl, x, c):
    return (yl % YL) * 8 + (x % X) * 2 + c % 2


def col_id(yh, z):
    return (yh % YH) * 8 + z % Z


def send_row(value, dyl, dx, dc):
    pairs = [
        (row_id(yl, x, c), row_id(yl + dyl, x + dx, c + dc))
        for yl in range(YL)
        for x in range(X)
        for c in range(2)
    ]
    return lax.ppermute(value, "row", pairs)


def send_col(value, dyh, dz):
    pairs = [
        (col_id(yh, z), col_id(yh + dyh, z + dz)) for yh in range(YH) for z in range(Z)
    ]
    return lax.ppermute(value, "col", pairs)


def gelu_value(v):
    cval = math.sqrt(2.0 / math.pi)
    return 0.5 * v * (1.0 + jnp.tanh(cval * (v + 0.044715 * v * v * v)))


def gelu_slope(v):
    cval = math.sqrt(2.0 / math.pi)
    tval = jnp.tanh(cval * (v + 0.044715 * v * v * v))
    return 0.5 * (1.0 + tval) + 0.5 * v * (1.0 - tval * tval) * cval * (
        1.0 + 3.0 * 0.044715 * v * v
    )


def times_transposed(left, right):
    return lax.dot_general(
        left, right, (((1,), (1,)), ((), ())), preferred_element_type=F32
    )


def over_tokens(left, right):
    return lax.dot_general(
        left, right, (((0,), (0,)), ((), ())), preferred_element_type=F32
    )


def rows_at(value, start, count):
    return lax.dynamic_slice_in_dim(value, start, count, axis=0)


def gather_z(own, pieces):
    blocks = [None] * Z
    blocks[0] = up = down = own
    half = own.shape[0] // 2
    for step in (1, 2, 3, 4):
        if step == 4:
            up, down = up[:half], down[half:]
        up, down = lax.optimization_barrier((up, down))
        up, down = send_col(up, 0, 1), send_col(down, 0, -1)
        if step == 2:
            up, down, pieces = lax.optimization_barrier((up, down, pieces))
        else:
            up, down = lax.optimization_barrier((up, down))
        blocks[Z - step], blocks[step] = up, down
    blocks[4] = jnp.concatenate([up, down], axis=0)
    return blocks, pieces


def scatter_z(part, beside):
    n = part(4).shape[0]
    half = n // 2
    far = part(4).astype(BF16)
    up, down, done = far[:half], far[half:], []
    for step in (4, 3, 2, 1):
        if step == 3:
            nothing = jnp.zeros((n - half, up.shape[1]), F32)
            up = jnp.concatenate([up.astype(F32), nothing], axis=0)
            down = jnp.concatenate([nothing, down.astype(F32)], axis=0)
        if step < 4:
            up = (part(step) + up).astype(BF16)
            down = (part(Z - step) + down).astype(BF16)
        up, down = lax.optimization_barrier((up, down))
        up, down = send_col(up, 0, 1), send_col(down, 0, -1)
        if beside:
            done.append(beside.pop(0)(*done))
        up, down, done = lax.optimization_barrier((up, down, done))
    return part(0) + up + down, done


def x_terms(value, x):
    n = value.shape[0] // X
    return [rows_at(value, (x + d) % X * n, n).astype(BF16) for d in (1, 2, 3)]


def scatter_x(value, x, terms):
    n = value.shape[0] // X
    total = rows_at(value, x * n, n)
    for d in (1, 3, 2):
        total += send_row(terms[d - 1], 0, d, 0)
    return total


def y_term(value, yl):
    n = value.shape[0] // YL
    return rows_at(value, (1 - yl) * n, n)


def scatter_y(value, yl, term):
    n = value.shape[0] // YL
    return rows_at(value, yl * n, n) + send_row(term, 1, 0, 0)


def gather_x(own):
    return [own] + [send_row(own, 0, -d, 0) for d in (1, 3, 2)]


def x_place(d):
    return d ^ (d >> 1)


def per_device(inputs, up_weight, down_weight, cotangent):
    row, col = lax.axis_index("row"), lax.axis_index("col")
    core, x, yl = row % 2, row // 2 % X, row // 8

    both = jnp.stack([inputs, cotangent]).reshape(2, 2, 16, 768)
    mine = lax.dynamic_index_in_dim(both, core, axis=1, keepdims=False)
    other = lax.dynamic_index_in_dim(both, 1 - core, axis=1, keepdims=False)
    here = jnp.concatenate([mine, send_row(other, 0, 0, 1)], axis=-1)
    there = send_col(here, 1, 0)
    shard = jnp.concatenate([here, there], axis=1)
    shard, up_own, down_own = lax.optimization_barrier((shard, up_weight, down_weight))

    up_all = jnp.concatenate([up_own, send_row(up_own, 0, 0, 1)], axis=0)
    down_all = jnp.concatenate([down_own, send_row(down_own, 0, 0, 1)], axis=1)
    blocks, (up_piece, down_piece) = gather_z(
        shard.reshape(64, 1536), (up_all[768:784], down_all[:16])
    )
    up_all = lax.dynamic_update_slice(up_all, up_piece, (768, 0))
    down_all = lax.dynamic_update_slice(down_all, down_piece, (0, 0))
    feats = jnp.concatenate([b[:32] for b in blocks], axis=0)
    cots = jnp.concatenate([b[32:] for b in blocks], axis=0)

    preact_part = jnp.dot(feats, up_all, preferred_element_type=F32)
    to_y = y_term(preact_part, yl).astype(BF16)
    act_part = times_transposed(cots, down_all)
    act_part = act_part.reshape(YL, X, 32, 1536).swapaxes(0, 1).reshape(256, 1536)
    to_x = x_terms(act_part, x)
    pre_half = scatter_y(preact_part, yl, to_y)
    act_half = scatter_x(act_part, x, to_x)
    preact = scatter_x(pre_half, x, x_terms(pre_half, x))
    act_grad = scatter_y(act_half, yl, y_term(act_half, yl))

    activ = gelu_value(preact).astype(BF16)
    pre_grad = (act_grad * gelu_slope(preact)).astype(BF16)

    across = jnp.concatenate(gather_x(activ), axis=0)
    pair = jnp.concatenate([pre_grad, send_row(pre_grad, 1, 0, 0)], axis=0)
    across, pair = lax.optimization_barrier((across, pair))
    pairs = gather_x(pair)
    pregrad_all = jnp.concatenate(pairs, axis=0)
    activ_all = jnp.concatenate([across, send_row(across, 1, 0, 0)], axis=0)

    def at_activ(d):
        return ((yl + d // X) % YL * X + x_place((d - x) % X)) * 32

    def at_pregrad(d):
        return (x_place((d - x) % X) * YL + (yl + d // X) % YL) * 32

    def out_rows(rows):
        return jnp.dot(rows, down_all, preferred_element_type=F32)

    def in_rows(rows):
        return times_transposed(rows, up_all)

    first_block = jnp.concatenate(
        [
            in_rows(rows_at(pregrad_all, at_pregrad(4), 32)),
            out_rows(rows_at(activ_all, at_activ(4), 32)),
        ],
        axis=0,
    )
    out_part = out_rows(activ_all)
    first_block, pair_rows = lax.optimization_barrier((first_block, pairs[0]))
    in_part = in_rows(jnp.concatenate([pair_rows] + pairs[1:], axis=0))

    def part(d):
        if d == 4:
            return first_block
        return jnp.concatenate(
            [
                rows_at(in_part, at_pregrad(d), 32),
                rows_at(out_part, at_activ(d), 32),
            ],
            axis=0,
        )

    def exchange():
        activ_in_order = [rows_at(activ_all, at_activ(d), 32) for d in range(Z)]
        pregrad_in_order = [rows_at(pregrad_all, at_pregrad(d), 32) for d in range(Z)]
        given = jnp.concatenate([feats[:, 768:], cots[:, 768:]], axis=1)
        given = jnp.concatenate([given] + activ_in_order + pregrad_in_order, axis=0)
        got = send_row(given, 0, 0, 1)
        return [
            jnp.concatenate([feats[:, :768], got[:256, :768]], axis=0),
            jnp.concatenate([cots[:, :768], got[:256, 768:]], axis=0),
            jnp.concatenate([given[256:512], got[256:512]], axis=0),
            jnp.concatenate([given[512:], got[512:]], axis=0),
        ]

    def down_gradient(tokens):
        return over_tokens(tokens[2], tokens[1]).astype(BF16)

    def up_gradient(tokens, down_grad):
        return over_tokens(tokens[0], tokens[3]).astype(BF16)

    total, (_, down_grad, up_grad) = scatter_z(
        part, [exchange, down_gradient, up_gradient]
    )
    total = total.reshape(2, 2, 16, 1536)
    total = total[:, 0] + send_col(total[:, 1].astype(BF16), 1, 0)
    mine = total[:, :, :768]
    other = send_row(total[:, :, 768:], 0, 0, 1)
    first = core == 0
    low = jnp.where(first, mine, other)
    high = jnp.where(first, other, mine)
    result = jnp.concatenate([low, high], axis=1).astype(BF16)
    return (result[1], result[0], up_grad, down_grad)


def solution(mesh):
    placed = (P("col", "row"), P("row", "col"), P("col", "row"), P("col", "row"))
    return jax.shard_map(
        per_device,
        mesh=mesh,
        in_specs=placed,
        out_specs=(P("col", "row"), P("col", "row"), P("row", "col"), P("col", "row")),
        check_vma=False,
    )
```

```python
import math

import jax
import jax.numpy as jnp
from jax import lax
from jax.sharding import PartitionSpec as P

BF16, F32 = jnp.bfloat16, jnp.float32
YL, X, YH, Z = 2, 4, 2, 8


def row_id(yl, x, c):
    return (yl % YL) * 8 + (x % X) * 2 + c % 2


def col_id(yh, z):
    return (yh % YH) * 8 + z % Z


def send_row(value, dyl, dx, dc):
    pairs = [
        (row_id(yl, x, c), row_id(yl + dyl, x + dx, c + dc))
        for yl in range(YL)
        for x in range(X)
        for c in range(2)
    ]
    return lax.ppermute(value, "row", pairs)


def send_col(value, dyh, dz):
    pairs = [
        (col_id(yh, z), col_id(yh + dyh, z + dz)) for yh in range(YH) for z in range(Z)
    ]
    return lax.ppermute(value, "col", pairs)


def gelu_value(v):
    cval = math.sqrt(2.0 / math.pi)
    return 0.5 * v * (1.0 + jnp.tanh(cval * (v + 0.044715 * v * v * v)))


def gelu_slope(v):
    cval = math.sqrt(2.0 / math.pi)
    tval = jnp.tanh(cval * (v + 0.044715 * v * v * v))
    return 0.5 * (1.0 + tval) + 0.5 * v * (1.0 - tval * tval) * cval * (
        1.0 + 3.0 * 0.044715 * v * v
    )


def times_transposed(left, right):
    return lax.dot_general(
        left, right, (((1,), (1,)), ((), ())), preferred_element_type=F32
    )


def over_tokens(left, right):
    return lax.dot_general(
        left, right, (((0,), (0,)), ((), ())), preferred_element_type=F32
    )


def rows_at(value, start, count):
    return lax.dynamic_slice_in_dim(value, start, count, axis=0)


def gather_z(own, pieces):
    blocks = [None] * Z
    blocks[0] = up = down = own
    half = own.shape[0] // 2
    for step in (1, 2, 3, 4):
        if step == 4:
            up, down = up[:half], down[half:]
        up, down = lax.optimization_barrier((up, down))
        up, down = send_col(up, 0, 1), send_col(down, 0, -1)
        if step == 2:
            up, down, pieces = lax.optimization_barrier((up, down, pieces))
        else:
            up, down = lax.optimization_barrier((up, down))
        blocks[Z - step], blocks[step] = up, down
    blocks[4] = jnp.concatenate([up, down], axis=0)
    return blocks, pieces


def scatter_z(part, beside):
    n = part(4).shape[0]
    half = n // 2
    far = part(4).astype(BF16)
    up, down, done = far[:half], far[half:], []
    for step in (4, 3, 2, 1):
        if step == 3:
            nothing = jnp.zeros((n - half, up.shape[1]), F32)
            up = jnp.concatenate([up.astype(F32), nothing], axis=0)
            down = jnp.concatenate([nothing, down.astype(F32)], axis=0)
        if step < 4:
            up = (part(step) + up).astype(BF16)
            down = (part(Z - step) + down).astype(BF16)
        up, down = lax.optimization_barrier((up, down))
        up, down = send_col(up, 0, 1), send_col(down, 0, -1)
        if beside:
            done.append(beside.pop(0)(*done))
        up, down, done = lax.optimization_barrier((up, down, done))
    return part(0) + up + down, done


def x_terms(value, x):
    n = value.shape[0] // X
    return [rows_at(value, (x + d) % X * n, n).astype(BF16) for d in (1, 2, 3)]


def scatter_x(value, x, terms):
    n = value.shape[0] // X
    total = rows_at(value, x * n, n)
    for d in (1, 3, 2):
        total += send_row(terms[d - 1], 0, d, 0)
    return total


def y_term(value, yl):
    n = value.shape[0] // YL
    return rows_at(value, (1 - yl) * n, n)


def scatter_y(value, yl, term):
    n = value.shape[0] // YL
    return rows_at(value, yl * n, n) + send_row(term, 1, 0, 0)


def gather_x(own):
    return [own] + [send_row(own, 0, -d, 0) for d in (1, 3, 2)]


def x_place(d):
    return d ^ (d >> 1)


def per_device(inputs, up_weight, down_weight, cotangent):
    row, col = lax.axis_index("row"), lax.axis_index("col")
    core, x, yl = row % 2, row // 2 % X, row // 8

    both = jnp.stack([inputs, cotangent]).reshape(2, 2, 16, 768)
    mine = lax.dynamic_index_in_dim(both, core, axis=1, keepdims=False)
    other = lax.dynamic_index_in_dim(both, 1 - core, axis=1, keepdims=False)
    here = jnp.concatenate([mine, send_row(other, 0, 0, 1)], axis=-1)
    there = send_col(here, 1, 0)
    shard = jnp.concatenate([here, there], axis=1)
    shard, up_own, down_own = lax.optimization_barrier((shard, up_weight, down_weight))

    up_all = jnp.concatenate([up_own, send_row(up_own, 0, 0, 1)], axis=0)
    down_all = jnp.concatenate([down_own, send_row(down_own, 0, 0, 1)], axis=1)
    blocks, (up_piece, down_piece) = gather_z(
        shard.reshape(64, 1536), (up_all[768:784], down_all[:16])
    )
    up_all = lax.dynamic_update_slice(up_all, up_piece, (768, 0))
    down_all = lax.dynamic_update_slice(down_all, down_piece, (0, 0))
    feats = jnp.concatenate([b[:32] for b in blocks], axis=0)
    cots = jnp.concatenate([b[32:] for b in blocks], axis=0)

    preact_part = jnp.dot(feats, up_all, preferred_element_type=F32)
    preact_part = preact_part.reshape(YL, X, 32, 1536).swapaxes(0, 1).reshape(256, 1536)
    pre_half = scatter_x(preact_part, x, x_terms(preact_part, x))
    preact = scatter_y(pre_half, yl, y_term(pre_half, yl))

    act_part = times_transposed(cots, down_all)
    act_half = scatter_y(act_part, yl, y_term(act_part, yl).astype(BF16))
    act_grad = scatter_x(act_half, x, x_terms(act_half, x))

    activ = gelu_value(preact).astype(BF16)
    pre_grad = (act_grad * gelu_slope(preact)).astype(BF16)

    across = jnp.concatenate(gather_x(activ), axis=0)
    pair = jnp.concatenate([pre_grad, send_row(pre_grad, 1, 0, 0)], axis=0)
    across, pair = lax.optimization_barrier((across, pair))
    pairs = gather_x(pair)
    pregrad_all = jnp.concatenate(pairs, axis=0)
    activ_all = jnp.concatenate([across, send_row(across, 1, 0, 0)], axis=0)

    def at_activ(d):
        return ((yl + d // X) % YL * X + x_place((d - x) % X)) * 32

    def at_pregrad(d):
        return (x_place((d - x) % X) * YL + (yl + d // X) % YL) * 32

    def out_rows(rows):
        return jnp.dot(rows, down_all, preferred_element_type=F32)

    def in_rows(rows):
        return times_transposed(rows, up_all)

    first_block = jnp.concatenate(
        [
            in_rows(rows_at(pregrad_all, at_pregrad(4), 32)),
            out_rows(rows_at(activ_all, at_activ(4), 32)),
        ],
        axis=0,
    )
    out_part = out_rows(activ_all)
    first_block, pair_rows = lax.optimization_barrier((first_block, pairs[0]))
    in_part = in_rows(jnp.concatenate([pair_rows] + pairs[1:], axis=0))

    def part(d):
        if d == 4:
            return first_block
        return jnp.concatenate(
            [
                rows_at(in_part, at_pregrad(d), 32),
                rows_at(out_part, at_activ(d), 32),
            ],
            axis=0,
        )

    def exchange():
        activ_in_order = [rows_at(activ_all, at_activ(d), 32) for d in range(Z)]
        pregrad_in_order = [rows_at(pregrad_all, at_pregrad(d), 32) for d in range(Z)]
        given = jnp.concatenate([feats[:, 768:], cots[:, 768:]], axis=1)
        given = jnp.concatenate([given] + activ_in_order + pregrad_in_order, axis=0)
        got = send_row(given, 0, 0, 1)
        return [
            jnp.concatenate([feats[:, :768], got[:256, :768]], axis=0),
            jnp.concatenate([cots[:, :768], got[:256, 768:]], axis=0),
            jnp.concatenate([given[256:512], got[256:512]], axis=0),
            jnp.concatenate([given[512:], got[512:]], axis=0),
        ]

    def down_gradient(tokens):
        return over_tokens(tokens[2], tokens[1]).astype(BF16)

    def up_gradient(tokens, down_grad):
        return over_tokens(tokens[0], tokens[3]).astype(BF16)

    total, (_, down_grad, up_grad) = scatter_z(
        part, [exchange, down_gradient, up_gradient]
    )
    total = total.reshape(2, 2, 16, 1536)
    total = total[:, 0] + send_col(total[:, 1].astype(BF16), 1, 0)
    mine = total[:, :, :768]
    other = send_row(total[:, :, 768:], 0, 0, 1)
    first = core == 0
    low = jnp.where(first, mine, other)
    high = jnp.where(first, other, mine)
    result = jnp.concatenate([low, high], axis=1).astype(BF16)
    return (result[1], result[0], up_grad, down_grad)


def solution(mesh):
    placed = (P("col", "row"), P("row", "col"), P("col", "row"), P("col", "row"))
    return jax.shard_map(
        per_device,
        mesh=mesh,
        in_specs=placed,
        out_specs=(P("col", "row"), P("col", "row"), P("row", "col"), P("col", "row")),
        check_vma=False,
    )
```

```python
import math

import jax
import jax.numpy as jnp
from jax import lax
from jax.sharding import PartitionSpec as P

BF16, F32 = jnp.bfloat16, jnp.float32
YL, X, YH, Z = 2, 4, 2, 8


def row_id(yl, x, c):
    return (yl % YL) * 8 + (x % X) * 2 + c % 2


def col_id(yh, z):
    return (yh % YH) * 8 + z % Z


def send_row(value, dyl, dx, dc):
    pairs = [
        (row_id(yl, x, c), row_id(yl + dyl, x + dx, c + dc))
        for yl in range(YL)
        for x in range(X)
        for c in range(2)
    ]
    return lax.ppermute(value, "row", pairs)


def send_col(value, dyh, dz):
    pairs = [
        (col_id(yh, z), col_id(yh + dyh, z + dz)) for yh in range(YH) for z in range(Z)
    ]
    return lax.ppermute(value, "col", pairs)


def gelu_value(v):
    cval = math.sqrt(2.0 / math.pi)
    return 0.5 * v * (1.0 + jnp.tanh(cval * (v + 0.044715 * v * v * v)))


def gelu_slope(v):
    cval = math.sqrt(2.0 / math.pi)
    tval = jnp.tanh(cval * (v + 0.044715 * v * v * v))
    return 0.5 * (1.0 + tval) + 0.5 * v * (1.0 - tval * tval) * cval * (
        1.0 + 3.0 * 0.044715 * v * v
    )


def times_transposed(left, right):
    return lax.dot_general(
        left, right, (((1,), (1,)), ((), ())), preferred_element_type=F32
    )


def over_tokens(left, right):
    return lax.dot_general(
        left, right, (((0,), (0,)), ((), ())), preferred_element_type=F32
    )


def rows_at(value, start, count):
    return lax.dynamic_slice_in_dim(value, start, count, axis=0)


def gather_z(own, pieces):
    blocks = [None] * Z
    blocks[0] = up = down = own
    half = own.shape[0] // 2
    for step in (1, 2, 3, 4):
        if step == 4:
            up, down = up[:half], down[half:]
        up, down = lax.optimization_barrier((up, down))
        up, down = send_col(up, 0, 1), send_col(down, 0, -1)
        if step == 2:
            up, down, pieces = lax.optimization_barrier((up, down, pieces))
        else:
            up, down = lax.optimization_barrier((up, down))
        blocks[Z - step], blocks[step] = up, down
    blocks[4] = jnp.concatenate([up, down], axis=0)
    return blocks, pieces


def scatter_z(part, beside):
    n = part(4).shape[0]
    half = n // 2
    far = part(4).astype(BF16)
    up, down, done = far[:half], far[half:], []
    for step in (4, 3, 2, 1):
        if step == 3:
            nothing = jnp.zeros((n - half, up.shape[1]), F32)
            up = jnp.concatenate([up.astype(F32), nothing], axis=0)
            down = jnp.concatenate([nothing, down.astype(F32)], axis=0)
        if step < 4:
            up = (part(step) + up).astype(BF16)
            down = (part(Z - step) + down).astype(BF16)
        up, down = lax.optimization_barrier((up, down))
        up, down = send_col(up, 0, 1), send_col(down, 0, -1)
        if beside:
            done.append(beside.pop(0)(*done))
        up, down, done = lax.optimization_barrier((up, down, done))
    return part(0) + up + down, done


def x_terms(value, x):
    n = value.shape[0] // X
    return [rows_at(value, (x + d) % X * n, n).astype(BF16) for d in (1, 2, 3)]


def scatter_x(value, x, terms):
    n = value.shape[0] // X
    total = rows_at(value, x * n, n)
    for d in (1, 3, 2):
        total += send_row(terms[d - 1], 0, d, 0)
    return total


def y_term(value, yl):
    n = value.shape[0] // YL
    return rows_at(value, (1 - yl) * n, n)


def scatter_y(value, yl, term):
    n = value.shape[0] // YL
    return rows_at(value, yl * n, n) + send_row(term, 1, 0, 0)


def gather_x(own):
    return [own] + [send_row(own, 0, -d, 0) for d in (1, 3, 2)]


def x_place(d):
    return d ^ (d >> 1)


def per_device(inputs, up_weight, down_weight, cotangent):
    row, col = lax.axis_index("row"), lax.axis_index("col")
    core, x, yl = row % 2, row // 2 % X, row // 8

    both = jnp.stack([inputs, cotangent]).reshape(2, 2, 16, 768)
    mine = lax.dynamic_index_in_dim(both, core, axis=1, keepdims=False)
    other = lax.dynamic_index_in_dim(both, 1 - core, axis=1, keepdims=False)
    here = jnp.concatenate([mine, send_row(other, 0, 0, 1)], axis=-1)
    there = send_col(here, 1, 0)
    shard = jnp.concatenate([here, there], axis=1)
    shard, up_own, down_own = lax.optimization_barrier((shard, up_weight, down_weight))

    up_all = jnp.concatenate([up_own, send_row(up_own, 0, 0, 1)], axis=0)
    down_all = jnp.concatenate([down_own, send_row(down_own, 0, 0, 1)], axis=1)
    blocks, (up_piece, down_piece) = gather_z(
        shard.reshape(64, 1536), (up_all[768:784], down_all[:16])
    )
    up_all = lax.dynamic_update_slice(up_all, up_piece, (768, 0))
    down_all = lax.dynamic_update_slice(down_all, down_piece, (0, 0))
    feats = jnp.concatenate([b[:32] for b in blocks], axis=0)
    cots = jnp.concatenate([b[32:] for b in blocks], axis=0)

    preact_part = jnp.dot(feats, up_all, preferred_element_type=F32)
    preact_part = preact_part.reshape(YL, X, 32, 1536).swapaxes(0, 1).reshape(256, 1536)
    pre_half = scatter_x(preact_part, x, x_terms(preact_part, x))
    preact = scatter_y(pre_half, yl, y_term(pre_half, yl))

    act_part = times_transposed(cots, down_all)
    act_half = scatter_y(act_part, yl, y_term(act_part, yl).astype(BF16))
    act_grad = scatter_x(act_half, x, x_terms(act_half, x))

    activ, slope = lax.optimization_barrier(
        (gelu_value(preact).astype(BF16), gelu_slope(preact))
    )
    pre_grad = (act_grad * slope).astype(BF16)

    across = jnp.concatenate(gather_x(activ), axis=0)
    pair = jnp.concatenate([pre_grad, send_row(pre_grad, 1, 0, 0)], axis=0)
    across, pair = lax.optimization_barrier((across, pair))
    pairs = gather_x(pair)
    pregrad_all = jnp.concatenate(pairs, axis=0)
    activ_all = jnp.concatenate([across, send_row(across, 1, 0, 0)], axis=0)

    def at_activ(d):
        return ((yl + d // X) % YL * X + x_place((d - x) % X)) * 32

    def at_pregrad(d):
        return (x_place((d - x) % X) * YL + (yl + d // X) % YL) * 32

    def out_rows(rows):
        return jnp.dot(rows, down_all, preferred_element_type=F32)

    def in_rows(rows):
        return times_transposed(rows, up_all)

    first_block = jnp.concatenate(
        [
            in_rows(rows_at(pregrad_all, at_pregrad(4), 32)),
            out_rows(rows_at(activ_all, at_activ(4), 32)),
        ],
        axis=0,
    )
    out_part = out_rows(activ_all)
    first_block, pair_rows = lax.optimization_barrier((first_block, pairs[0]))
    in_part = in_rows(jnp.concatenate([pair_rows] + pairs[1:], axis=0))

    def part(d):
        if d == 4:
            return first_block
        return jnp.concatenate(
            [
                rows_at(in_part, at_pregrad(d), 32),
                rows_at(out_part, at_activ(d), 32),
            ],
            axis=0,
        )

    def exchange():
        activ_in_order = [rows_at(activ_all, at_activ(d), 32) for d in range(Z)]
        pregrad_in_order = [rows_at(pregrad_all, at_pregrad(d), 32) for d in range(Z)]
        given = jnp.concatenate([feats[:, 768:], cots[:, 768:]], axis=1)
        given = jnp.concatenate([given] + activ_in_order + pregrad_in_order, axis=0)
        got = send_row(given, 0, 0, 1)
        return [
            jnp.concatenate([feats[:, :768], got[:256, :768]], axis=0),
            jnp.concatenate([cots[:, :768], got[:256, 768:]], axis=0),
            jnp.concatenate([given[256:512], got[256:512]], axis=0),
            jnp.concatenate([given[512:], got[512:]], axis=0),
        ]

    def down_gradient(tokens):
        return over_tokens(tokens[2], tokens[1]).astype(BF16)

    def up_gradient(tokens, down_grad):
        return over_tokens(tokens[0], tokens[3]).astype(BF16)

    total, (_, down_grad, up_grad) = scatter_z(
        part, [exchange, down_gradient, up_gradient]
    )
    total = total.reshape(2, 2, 16, 1536)
    total = total[:, 0] + send_col(total[:, 1].astype(BF16), 1, 0)
    mine = total[:, :, :768]
    other = send_row(total[:, :, 768:], 0, 0, 1)
    first = core == 0
    low = jnp.where(first, mine, other)
    high = jnp.where(first, other, mine)
    result = jnp.concatenate([low, high], axis=1).astype(BF16)
    return (result[1], result[0], up_grad, down_grad)


def solution(mesh):
    placed = (P("col", "row"), P("row", "col"), P("col", "row"), P("col", "row"))
    return jax.shard_map(
        per_device,
        mesh=mesh,
        in_specs=placed,
        out_specs=(P("col", "row"), P("col", "row"), P("row", "col"), P("col", "row")),
        check_vma=False,
    )
```

```python
import math

import jax
import jax.numpy as jnp
from jax import lax
from jax.sharding import PartitionSpec as P

BF16, F32 = jnp.bfloat16, jnp.float32
YL, X, YH, Z = 2, 4, 2, 8


def row_id(yl, x, c):
    return (yl % YL) * 8 + (x % X) * 2 + c % 2


def col_id(yh, z):
    return (yh % YH) * 8 + z % Z


def send_row(value, dyl, dx, dc):
    pairs = [
        (row_id(yl, x, c), row_id(yl + dyl, x + dx, c + dc))
        for yl in range(YL)
        for x in range(X)
        for c in range(2)
    ]
    return lax.ppermute(value, "row", pairs)


def send_col(value, dyh, dz):
    pairs = [
        (col_id(yh, z), col_id(yh + dyh, z + dz)) for yh in range(YH) for z in range(Z)
    ]
    return lax.ppermute(value, "col", pairs)


def gelu_value(v):
    cval = math.sqrt(2.0 / math.pi)
    return 0.5 * v * (1.0 + jnp.tanh(cval * (v + 0.044715 * v * v * v)))


def gelu_slope(v):
    cval = math.sqrt(2.0 / math.pi)
    tval = jnp.tanh(cval * (v + 0.044715 * v * v * v))
    return 0.5 * (1.0 + tval) + 0.5 * v * (1.0 - tval * tval) * cval * (
        1.0 + 3.0 * 0.044715 * v * v
    )


def times_transposed(left, right):
    return lax.dot_general(
        left, right, (((1,), (1,)), ((), ())), preferred_element_type=F32
    )


def over_tokens(left, right):
    return lax.dot_general(
        left, right, (((0,), (0,)), ((), ())), preferred_element_type=F32
    )


def rows_at(value, start, count):
    return lax.dynamic_slice_in_dim(value, start, count, axis=0)


def gather_z(own, pieces):
    blocks = [None] * Z
    blocks[0] = up = down = own
    half = own.shape[0] // 2
    for step in (1, 2, 3, 4):
        if step == 4:
            up, down = up[:half], down[half:]
        up, down = lax.optimization_barrier((up, down))
        up, down = send_col(up, 0, 1), send_col(down, 0, -1)
        if step == 2:
            up, down, pieces = lax.optimization_barrier((up, down, pieces))
        else:
            up, down = lax.optimization_barrier((up, down))
        blocks[Z - step], blocks[step] = up, down
    blocks[4] = jnp.concatenate([up, down], axis=0)
    return blocks, pieces


def scatter_z(part, beside):
    n = part(4).shape[0]
    half = n // 2
    far = part(4).astype(BF16)
    up, down, done = far[:half], far[half:], []
    for step in (4, 3, 2, 1):
        if step == 3:
            nothing = jnp.zeros((n - half, up.shape[1]), F32)
            up = jnp.concatenate([up.astype(F32), nothing], axis=0)
            down = jnp.concatenate([nothing, down.astype(F32)], axis=0)
        if step < 4:
            up = (part(step) + up).astype(BF16)
            down = (part(Z - step) + down).astype(BF16)
        up, down = lax.optimization_barrier((up, down))
        up, down = send_col(up, 0, 1), send_col(down, 0, -1)
        if beside:
            done.append(beside.pop(0)(*done))
        up, down, done = lax.optimization_barrier((up, down, done))
    return part(0) + up + down, done


def x_terms(value, x):
    n = value.shape[0] // X
    return [rows_at(value, (x + d) % X * n, n).astype(BF16) for d in (1, 2, 3)]


def scatter_x(value, x, terms):
    n = value.shape[0] // X
    total = rows_at(value, x * n, n)
    for d in (1, 3, 2):
        total += send_row(terms[d - 1], 0, d, 0)
    return total


def y_term(value, yl):
    n = value.shape[0] // YL
    return rows_at(value, (1 - yl) * n, n)


def scatter_y(value, yl, term):
    n = value.shape[0] // YL
    return rows_at(value, yl * n, n) + send_row(term, 1, 0, 0)


def gather_x(own, order):
    return [own] + [send_row(own, 0, -d, 0) for d in order]


def per_device(inputs, up_weight, down_weight, cotangent):
    row, col = lax.axis_index("row"), lax.axis_index("col")
    core, x, yl = row % 2, row // 2 % X, row // 8

    both = jnp.stack([inputs, cotangent]).reshape(2, 2, 16, 768)
    mine = lax.dynamic_index_in_dim(both, core, axis=1, keepdims=False)
    other = lax.dynamic_index_in_dim(both, 1 - core, axis=1, keepdims=False)
    here = jnp.concatenate([mine, send_row(other, 0, 0, 1)], axis=-1)
    there = send_col(here, 1, 0)
    shard = jnp.concatenate([here, there], axis=1)
    shard, up_own, down_own = lax.optimization_barrier((shard, up_weight, down_weight))

    up_all = jnp.concatenate([up_own, send_row(up_own, 0, 0, 1)], axis=0)
    down_all = jnp.concatenate([down_own, send_row(down_own, 0, 0, 1)], axis=1)
    blocks, (up_piece, down_piece) = gather_z(
        shard.reshape(64, 1536), (up_all[768:784], down_all[:16])
    )
    up_all = lax.dynamic_update_slice(up_all, up_piece, (768, 0))
    down_all = lax.dynamic_update_slice(down_all, down_piece, (0, 0))
    feats = jnp.concatenate([b[:32] for b in blocks], axis=0)
    cots = jnp.concatenate([b[32:] for b in blocks], axis=0)

    preact_part = jnp.dot(feats, up_all, preferred_element_type=F32)
    preact_part = preact_part.reshape(YL, X, 32, 1536).swapaxes(0, 1).reshape(256, 1536)
    pre_half = scatter_x(preact_part, x, x_terms(preact_part, x))
    preact = scatter_y(pre_half, yl, y_term(pre_half, yl))

    act_part = times_transposed(cots, down_all)
    act_half = scatter_y(act_part, yl, y_term(act_part, yl).astype(BF16))
    act_grad = scatter_x(act_half, x, x_terms(act_half, x))

    activ, slope = lax.optimization_barrier(
        (gelu_value(preact).astype(BF16), gelu_slope(preact))
    )
    pre_grad = (act_grad * slope).astype(BF16)

    across = jnp.concatenate(gather_x(activ, (2, 1, 3)), axis=0)
    pair = jnp.concatenate([pre_grad, send_row(pre_grad, 1, 0, 0)], axis=0)
    pairs = gather_x(pair, (1, 3, 2))
    pregrad_all = jnp.concatenate(pairs, axis=0)
    activ_all = jnp.concatenate([across, send_row(across, 1, 0, 0)], axis=0)

    def at_activ(d):
        far = (d - x) % X
        return ((yl + d // X) % YL * X + far % 2 * 2 + far // 2) * 32

    def at_pregrad(d):
        far = (d - x) % X
        return ((far ^ (far >> 1)) * YL + (yl + d // X) % YL) * 32

    def out_rows(rows):
        return jnp.dot(rows, down_all, preferred_element_type=F32)

    def in_rows(rows):
        return times_transposed(rows, up_all)

    first_block = jnp.concatenate(
        [
            in_rows(rows_at(pregrad_all, at_pregrad(4), 32)),
            out_rows(rows_at(activ_all, at_activ(4), 32)),
        ],
        axis=0,
    )
    out_part = out_rows(activ_all)
    first_block, pair_rows = lax.optimization_barrier((first_block, pairs[0]))
    in_part = in_rows(jnp.concatenate([pair_rows] + pairs[1:], axis=0))

    def part(d):
        if d == 4:
            return first_block
        return jnp.concatenate(
            [
                rows_at(in_part, at_pregrad(d), 32),
                rows_at(out_part, at_activ(d), 32),
            ],
            axis=0,
        )

    def exchange():
        activ_in_order = [rows_at(activ_all, at_activ(d), 32) for d in range(Z)]
        pregrad_in_order = [rows_at(pregrad_all, at_pregrad(d), 32) for d in range(Z)]
        given = jnp.concatenate([feats[:, 768:], cots[:, 768:]], axis=1)
        given = jnp.concatenate([given] + activ_in_order + pregrad_in_order, axis=0)
        got = send_row(given, 0, 0, 1)
        return [
            jnp.concatenate([feats[:, :768], got[:256, :768]], axis=0),
            jnp.concatenate([cots[:, :768], got[:256, 768:]], axis=0),
            jnp.concatenate([given[256:512], got[256:512]], axis=0),
            jnp.concatenate([given[512:], got[512:]], axis=0),
        ]

    def down_gradient(tokens):
        return over_tokens(tokens[2], tokens[1]).astype(BF16)

    def up_gradient(tokens, down_grad):
        return over_tokens(tokens[0], tokens[3]).astype(BF16)

    total, (_, down_grad, up_grad) = scatter_z(
        part, [exchange, down_gradient, up_gradient]
    )
    total = total.reshape(2, 2, 16, 1536)
    total = total[:, 0] + send_col(total[:, 1].astype(BF16), 1, 0)
    mine = total[:, :, :768]
    other = send_row(total[:, :, 768:], 0, 0, 1)
    first = core == 0
    low = jnp.where(first, mine, other)
    high = jnp.where(first, other, mine)
    result = jnp.concatenate([low, high], axis=1).astype(BF16)
    return (result[1], result[0], up_grad, down_grad)


def solution(mesh):
    placed = (P("col", "row"), P("row", "col"), P("col", "row"), P("col", "row"))
    return jax.shard_map(
        per_device,
        mesh=mesh,
        in_specs=placed,
        out_specs=(P("col", "row"), P("col", "row"), P("row", "col"), P("col", "row")),
        check_vma=False,
    )
```

```python
import math

import jax
import jax.numpy as jnp
from jax import lax
from jax.sharding import PartitionSpec as P

BF16, F32 = jnp.bfloat16, jnp.float32
YL, X, YH, Z = 2, 4, 2, 8


def row_id(yl, x, c):
    return (yl % YL) * 8 + (x % X) * 2 + c % 2


def col_id(yh, z):
    return (yh % YH) * 8 + z % Z


def send_row(value, dyl, dx, dc):
    pairs = [
        (row_id(yl, x, c), row_id(yl + dyl, x + dx, c + dc))
        for yl in range(YL)
        for x in range(X)
        for c in range(2)
    ]
    return lax.ppermute(value, "row", pairs)


def send_col(value, dyh, dz):
    pairs = [
        (col_id(yh, z), col_id(yh + dyh, z + dz)) for yh in range(YH) for z in range(Z)
    ]
    return lax.ppermute(value, "col", pairs)


def gelu_value(v):
    cval = math.sqrt(2.0 / math.pi)
    return 0.5 * v * (1.0 + jnp.tanh(cval * (v + 0.044715 * v * v * v)))


def gelu_slope(v):
    cval = math.sqrt(2.0 / math.pi)
    tval = jnp.tanh(cval * (v + 0.044715 * v * v * v))
    return 0.5 * (1.0 + tval) + 0.5 * v * (1.0 - tval * tval) * cval * (
        1.0 + 3.0 * 0.044715 * v * v
    )


def times_transposed(left, right):
    return lax.dot_general(
        left, right, (((1,), (1,)), ((), ())), preferred_element_type=F32
    )


def over_tokens(left, right):
    return lax.dot_general(
        left, right, (((0,), (0,)), ((), ())), preferred_element_type=F32
    )


def rows_at(value, start, count):
    return lax.dynamic_slice_in_dim(value, start, count, axis=0)


def gather_z(own, pieces):
    blocks = [None] * Z
    blocks[0] = up = down = own
    half = own.shape[0] // 2
    for step in (1, 2, 3, 4):
        if step == 4:
            up, down = up[:half], down[half:]
        up, down = lax.optimization_barrier((up, down))
        up, down = send_col(up, 0, 1), send_col(down, 0, -1)
        if step == 2:
            up, down, pieces = lax.optimization_barrier((up, down, pieces))
        else:
            up, down = lax.optimization_barrier((up, down))
        blocks[Z - step], blocks[step] = up, down
    blocks[4] = jnp.concatenate([up, down], axis=0)
    return blocks, pieces


def scatter_z(part, beside):
    n = part(4).shape[0]
    half = n // 2
    far = part(4).astype(BF16)
    up, down, done = far[:half], far[half:], []
    for step in (4, 3, 2, 1):
        if step == 3:
            nothing = jnp.zeros((n - half, up.shape[1]), F32)
            up = jnp.concatenate([up.astype(F32), nothing], axis=0)
            down = jnp.concatenate([nothing, down.astype(F32)], axis=0)
        if step < 4:
            up = (part(step) + up).astype(BF16)
            down = (part(Z - step) + down).astype(BF16)
        up, down = lax.optimization_barrier((up, down))
        up, down = send_col(up, 0, 1), send_col(down, 0, -1)
        if beside:
            done.append(beside.pop(0)(*done))
        up, down, done = lax.optimization_barrier((up, down, done))
    return part(0) + up + down, done


def x_terms(value, x):
    n = value.shape[0] // X
    return [rows_at(value, (x + d) % X * n, n).astype(BF16) for d in (1, 2, 3)]


def scatter_x(value, x, terms):
    n = value.shape[0] // X
    total = rows_at(value, x * n, n)
    for d in (1, 3, 2):
        total += send_row(terms[d - 1], 0, d, 0)
    return total


def y_term(value, yl):
    n = value.shape[0] // YL
    return rows_at(value, (1 - yl) * n, n)


def scatter_y(value, yl, term):
    n = value.shape[0] // YL
    return rows_at(value, yl * n, n) + send_row(term, 1, 0, 0)


def gather_x(own, order):
    return [own] + [send_row(own, 0, -d, 0) for d in order]


def per_device(inputs, up_weight, down_weight, cotangent):
    row, col = lax.axis_index("row"), lax.axis_index("col")
    core, x, yl = row % 2, row // 2 % X, row // 8

    both = jnp.stack([inputs, cotangent]).reshape(2, 2, 16, 768)
    mine = lax.dynamic_index_in_dim(both, core, axis=1, keepdims=False)
    other = lax.dynamic_index_in_dim(both, 1 - core, axis=1, keepdims=False)
    here = jnp.concatenate([mine, send_row(other, 0, 0, 1)], axis=-1)
    there = send_col(here, 1, 0)
    shard = jnp.concatenate([here, there], axis=1)
    shard, up_own, down_own = lax.optimization_barrier((shard, up_weight, down_weight))

    up_all = jnp.concatenate([up_own, send_row(up_own, 0, 0, 1)], axis=0)
    down_all = jnp.concatenate([down_own, send_row(down_own, 0, 0, 1)], axis=1)
    blocks, (up_piece, down_piece) = gather_z(
        shard.reshape(64, 1536), (up_all[768:784], down_all[:16])
    )
    up_all = lax.dynamic_update_slice(up_all, up_piece, (768, 0))
    down_all = lax.dynamic_update_slice(down_all, down_piece, (0, 0))
    feats = jnp.concatenate([b[:32] for b in blocks], axis=0)
    cots = jnp.concatenate([b[32:] for b in blocks], axis=0)

    preact_part = jnp.dot(feats, up_all, preferred_element_type=F32)
    preact_part = preact_part.reshape(YL, X, 32, 1536).swapaxes(0, 1).reshape(256, 1536)
    pre_half = scatter_x(preact_part, x, x_terms(preact_part, x))
    preact = scatter_y(pre_half, yl, y_term(pre_half, yl))

    act_part = times_transposed(cots, down_all)
    act_half = scatter_y(act_part, yl, y_term(act_part, yl).astype(BF16))
    act_grad = scatter_x(act_half, x, x_terms(act_half, x))

    activ, slope = lax.optimization_barrier(
        (gelu_value(preact).astype(BF16), gelu_slope(preact))
    )
    pre_grad = (act_grad * slope).astype(BF16)

    across = jnp.concatenate(gather_x(activ, (2, 1, 3)), axis=0)
    pair = jnp.concatenate([pre_grad, send_row(pre_grad, 1, 0, 0)], axis=0)
    pairs = gather_x(pair, (1, 3, 2))
    pregrad_all = jnp.concatenate(pairs, axis=0)
    activ_all = jnp.concatenate([across, send_row(across, 1, 0, 0)], axis=0)

    def at_activ(d):
        far = (d - x) % X
        return ((yl + d // X) % YL * X + far % 2 * 2 + far // 2) * 32

    def at_pregrad(d):
        far = (d - x) % X
        return ((far ^ (far >> 1)) * YL + (yl + d // X) % YL) * 32

    def out_rows(rows):
        return jnp.dot(rows, down_all, preferred_element_type=F32)

    def in_rows(rows):
        return times_transposed(rows, up_all)

    first_block = jnp.concatenate(
        [
            in_rows(rows_at(pregrad_all, at_pregrad(4), 32)),
            out_rows(rows_at(activ_all, at_activ(4), 32)),
        ],
        axis=0,
    )
    out_part = out_rows(activ_all)
    first_block, pair_rows = lax.optimization_barrier((first_block, pairs[0]))
    in_part = in_rows(jnp.concatenate([pair_rows] + pairs[1:], axis=0))

    def part(d):
        if d == 4:
            return first_block
        return jnp.concatenate(
            [
                rows_at(in_part, at_pregrad(d), 32),
                rows_at(out_part, at_activ(d), 32),
            ],
            axis=0,
        )

    def exchange():
        activ_in_order = [rows_at(activ_all, at_activ(d), 32) for d in range(Z)]
        pregrad_in_order = [rows_at(pregrad_all, at_pregrad(d), 32) for d in range(Z)]
        given = jnp.concatenate([feats[:, 768:], cots[:, 768:]], axis=1)
        given = jnp.concatenate([given] + activ_in_order + pregrad_in_order, axis=0)
        got = send_row(given, 0, 0, 1)
        return [
            jnp.concatenate([feats[:, :768], got[:256, :768]], axis=0),
            jnp.concatenate([cots[:, :768], got[:256, 768:]], axis=0),
            jnp.concatenate([given[256:512], got[256:512]], axis=0),
            jnp.concatenate([given[512:], got[512:]], axis=0),
        ]

    def down_gradient(tokens):
        return over_tokens(tokens[2], tokens[1]).astype(BF16)

    def up_gradient(tokens, down_grad):
        return over_tokens(tokens[0], tokens[3]).astype(BF16)

    total, (_, down_grad, up_grad) = scatter_z(
        part, [exchange, down_gradient, up_gradient]
    )
    total = total.reshape(2, 2, 16, 1536)
    total = total[:, 0] + send_col(total[:, 1], 1, 0)
    mine = total[:, :, :768]
    other = send_row(total[:, :, 768:], 0, 0, 1)
    first = core == 0
    low = jnp.where(first, mine, other)
    high = jnp.where(first, other, mine)
    result = jnp.concatenate([low, high], axis=1).astype(BF16)
    return (result[1], result[0], up_grad, down_grad)


def solution(mesh):
    placed = (P("col", "row"), P("row", "col"), P("col", "row"), P("col", "row"))
    return jax.shard_map(
        per_device,
        mesh=mesh,
        in_specs=placed,
        out_specs=(P("col", "row"), P("col", "row"), P("row", "col"), P("col", "row")),
        check_vma=False,
    )
```

```python
import math

import jax
import jax.numpy as jnp
from jax import lax
from jax.sharding import PartitionSpec as P

BF16, F32 = jnp.bfloat16, jnp.float32
YL, X, YH, Z = 2, 4, 2, 8


def row_id(yl, x, c):
    return (yl % YL) * 8 + (x % X) * 2 + c % 2


def col_id(yh, z):
    return (yh % YH) * 8 + z % Z


def send_row(value, dyl, dx, dc):
    pairs = [
        (row_id(yl, x, c), row_id(yl + dyl, x + dx, c + dc))
        for yl in range(YL)
        for x in range(X)
        for c in range(2)
    ]
    return lax.ppermute(value, "row", pairs)


def send_col(value, dyh, dz):
    pairs = [
        (col_id(yh, z), col_id(yh + dyh, z + dz)) for yh in range(YH) for z in range(Z)
    ]
    return lax.ppermute(value, "col", pairs)


def gelu_value(v):
    cval = math.sqrt(2.0 / math.pi)
    return 0.5 * v * (1.0 + jnp.tanh(cval * (v + 0.044715 * v * v * v)))


def gelu_slope(v):
    cval = math.sqrt(2.0 / math.pi)
    tval = jnp.tanh(cval * (v + 0.044715 * v * v * v))
    return 0.5 * (1.0 + tval) + 0.5 * v * (1.0 - tval * tval) * cval * (
        1.0 + 3.0 * 0.044715 * v * v
    )


def times_transposed(left, right):
    return lax.dot_general(
        left, right, (((1,), (1,)), ((), ())), preferred_element_type=F32
    )


def over_tokens(left, right):
    return lax.dot_general(
        left, right, (((0,), (0,)), ((), ())), preferred_element_type=F32
    )


def rows_at(value, start, count):
    return lax.dynamic_slice_in_dim(value, start, count, axis=0)


def gather_z(own, pieces):
    blocks = [None] * Z
    blocks[0] = up = down = own
    half = own.shape[0] // 2
    for step in (1, 2, 3, 4):
        if step == 4:
            up, down = up[:half], down[half:]
        up, down = lax.optimization_barrier((up, down))
        up, down = send_col(up, 0, 1), send_col(down, 0, -1)
        if step == 2:
            up, down, pieces = lax.optimization_barrier((up, down, pieces))
        else:
            up, down = lax.optimization_barrier((up, down))
        blocks[Z - step], blocks[step] = up, down
    blocks[4] = jnp.concatenate([up, down], axis=0)
    return blocks, pieces


def scatter_z(part, beside):
    n = part(4).shape[0]
    half = n // 2
    far = part(4).astype(BF16)
    up, down, done = far[:half], far[half:], []
    for step in (4, 3, 2, 1):
        if step == 3:
            nothing = jnp.zeros((n - half, up.shape[1]), F32)
            up = jnp.concatenate([up.astype(F32), nothing], axis=0)
            down = jnp.concatenate([nothing, down.astype(F32)], axis=0)
        if step < 4:
            up = (part(step) + up).astype(BF16)
            down = (part(Z - step) + down).astype(BF16)
        up, down = lax.optimization_barrier((up, down))
        up, down = send_col(up, 0, 1), send_col(down, 0, -1)
        if beside:
            done.append(beside.pop(0)(*done))
        up, down, done = lax.optimization_barrier((up, down, done))
    return part(0) + up + down, done


def x_terms(value, x):
    n = value.shape[0] // X
    return [rows_at(value, (x + d) % X * n, n).astype(BF16) for d in (1, 2, 3)]


def scatter_x(value, x, terms):
    n = value.shape[0] // X
    total = rows_at(value, x * n, n)
    for d in (1, 3, 2):
        total += send_row(terms[d - 1], 0, d, 0)
    return total


def y_term(value, yl):
    n = value.shape[0] // YL
    return rows_at(value, (1 - yl) * n, n)


def scatter_y(value, yl, term):
    n = value.shape[0] // YL
    return rows_at(value, yl * n, n) + send_row(term, 1, 0, 0)


def gather_x(own, order):
    return [own] + [send_row(own, 0, -d, 0) for d in order]


def per_device(inputs, up_weight, down_weight, cotangent):
    row, col = lax.axis_index("row"), lax.axis_index("col")
    core, x, yl = row % 2, row // 2 % X, row // 8

    both = jnp.stack([inputs, cotangent]).reshape(2, 2, 16, 768)
    mine = lax.dynamic_index_in_dim(both, core, axis=1, keepdims=False)
    other = lax.dynamic_index_in_dim(both, 1 - core, axis=1, keepdims=False)
    here = jnp.concatenate([mine, send_row(other, 0, 0, 1)], axis=-1)
    there = send_col(here, 1, 0)
    shard = jnp.concatenate([here, there], axis=1)
    shard, up_own, down_own = lax.optimization_barrier((shard, up_weight, down_weight))

    up_all = jnp.concatenate([up_own, send_row(up_own, 0, 0, 1)], axis=0)
    down_all = jnp.concatenate([down_own, send_row(down_own, 0, 0, 1)], axis=1)
    blocks, (up_piece, down_piece) = gather_z(
        shard.reshape(64, 1536), (up_all[768:784], down_all[:16])
    )
    up_all = lax.dynamic_update_slice(up_all, up_piece, (768, 0))
    down_all = lax.dynamic_update_slice(down_all, down_piece, (0, 0))
    feats = jnp.concatenate([b[:32] for b in blocks], axis=0)
    cots = jnp.concatenate([b[32:] for b in blocks], axis=0)

    preact_part = jnp.dot(feats, up_all, preferred_element_type=F32)
    preact_part = preact_part.reshape(YL, X, 32, 1536).swapaxes(0, 1).reshape(256, 1536)
    pre_half = scatter_x(preact_part, x, x_terms(preact_part, x))
    preact = scatter_y(pre_half, yl, y_term(pre_half, yl))

    act_part = times_transposed(cots, down_all)
    act_half = scatter_y(act_part, yl, y_term(act_part, yl).astype(BF16))
    act_grad = scatter_x(act_half, x, x_terms(act_half, x))

    activ, slope = lax.optimization_barrier(
        (gelu_value(preact).astype(BF16), gelu_slope(preact))
    )
    pre_grad = (act_grad * slope).astype(BF16)

    across = jnp.concatenate(gather_x(activ, (2, 1, 3)), axis=0)
    pair = jnp.concatenate([pre_grad, send_row(pre_grad, 1, 0, 0)], axis=0)
    pairs = gather_x(pair, (1, 3, 2))
    pregrad_all = jnp.concatenate(pairs, axis=0)
    activ_all = jnp.concatenate([across, send_row(across, 1, 0, 0)], axis=0)

    def at_activ(d):
        far = (d - x) % X
        return ((yl + d // X) % YL * X + far % 2 * 2 + far // 2) * 32

    def at_pregrad(d):
        far = (d - x) % X
        return ((far ^ (far >> 1)) * YL + (yl + d // X) % YL) * 32

    def out_rows(rows):
        return jnp.dot(rows, down_all, preferred_element_type=F32)

    def in_rows(rows):
        return times_transposed(rows, up_all)

    in_part = in_rows(pregrad_all)
    first_block = jnp.concatenate(
        [
            rows_at(in_part, at_pregrad(4), 32),
            out_rows(rows_at(activ_all, at_activ(4), 32)),
        ],
        axis=0,
    )
    out_part = out_rows(activ_all)

    def part(d):
        if d == 4:
            return first_block
        return jnp.concatenate(
            [
                rows_at(in_part, at_pregrad(d), 32),
                rows_at(out_part, at_activ(d), 32),
            ],
            axis=0,
        )

    def exchange():
        activ_in_order = [rows_at(activ_all, at_activ(d), 32) for d in range(Z)]
        pregrad_in_order = [rows_at(pregrad_all, at_pregrad(d), 32) for d in range(Z)]
        given = jnp.concatenate([feats[:, 768:], cots[:, 768:]], axis=1)
        given = jnp.concatenate([given] + activ_in_order + pregrad_in_order, axis=0)
        got = send_row(given, 0, 0, 1)
        return [
            jnp.concatenate([feats[:, :768], got[:256, :768]], axis=0),
            jnp.concatenate([cots[:, :768], got[:256, 768:]], axis=0),
            jnp.concatenate([given[256:512], got[256:512]], axis=0),
            jnp.concatenate([given[512:], got[512:]], axis=0),
        ]

    def down_gradient(tokens):
        return over_tokens(tokens[2], tokens[1]).astype(BF16)

    def up_gradient(tokens, down_grad):
        return over_tokens(tokens[0], tokens[3]).astype(BF16)

    total, (_, down_grad, up_grad) = scatter_z(
        part, [exchange, down_gradient, up_gradient]
    )
    total = total.reshape(2, 2, 16, 1536)
    total = total[:, 0] + send_col(total[:, 1].astype(BF16), 1, 0)
    mine = total[:, :, :768]
    other = send_row(total[:, :, 768:], 0, 0, 1)
    first = core == 0
    low = jnp.where(first, mine, other)
    high = jnp.where(first, other, mine)
    result = jnp.concatenate([low, high], axis=1).astype(BF16)
    return (result[1], result[0], up_grad, down_grad)


def solution(mesh):
    placed = (P("col", "row"), P("row", "col"), P("col", "row"), P("col", "row"))
    return jax.shard_map(
        per_device,
        mesh=mesh,
        in_specs=placed,
        out_specs=(P("col", "row"), P("col", "row"), P("row", "col"), P("col", "row")),
        check_vma=False,
    )
```
